512 devices in a mesh: group: 4 (over x_lo, core), blk: 16 (over z), local: 8 (over x_hi, y).
Axes of the slice: x: 4 (x_hi: 2, x_lo: 2; x = x_hi * 2 + x_lo), y: 4, z: 16, core: 2. Of those that a mesh axis runs over, the one named last changes fastest.
Arguments:
- tokens: bfloat16 [12288, 2048], P(('group', 'blk'), 'local'), may hold values from -6 to 6
- d_out: bfloat16 [12288, 2048], P(('group', 'blk'), 'local'), may hold values from -6 to 6
- ids: int32 [12288, 2], P(('group', 'blk')), may hold values from 0 to 7, all different within a row; in each aligned block of 192 rows (0 to 191, 192 to 383, ...) at most 64 rows name the same one
- gates: float32 [12288, 2], P(('group', 'blk')), may hold values from 0.1 to 1
- w_gate: bfloat16 [8, 2048, 1024], P('group', 'blk', 'local'), may hold values from -0.125 to 0.125
- w_up: bfloat16 [8, 2048, 1024], P('group', 'blk', 'local'), may hold values from -0.125 to 0.125
- w_down: bfloat16 [8, 1024, 2048], P('group', 'local', 'blk'), may hold values from -0.1875 to 0.1875
Outputs:
- moe_out: bfloat16 [12288, 2048], P(('group', 'blk'), 'local')
- grad_tokens: bfloat16 [12288, 2048], P(('group', 'blk'), 'local')
- grad_gates: float32 [12288, 2], P(('group', 'blk'))
- grad_gate: float32 [8, 2048, 1024], P('group', 'blk', 'local')
- grad_up: float32 [8, 2048, 1024], P('group', 'blk', 'local')
- grad_down: float32 [8, 1024, 2048], P('group', 'local', 'blk')
The draws below stay inside these ranges and needn't reach their ends.
Inputs may be any that keep to these rules, and one draw needn't show every extreme that they name: `ids`: each row names 2 different experts; among the 192 rows of one block an expert is named by at most 64 rows, a bound that some block reaches; every expert is named somewhere.
All inputs are finite; a program needn't handle non-finite values.
Results may differ from the reference program's by a relative error of at most 0.02.
Values may be sent and summed in bfloat16 or wider, within the bound.
A program may use at most 64 MiB of HBM per device.

```python
import math
import jax
import jax.numpy as jnp
import numpy as np
from jax import lax

D = 2048
FF = 1024
TOP = 2
TOK_POS = 192
EXPERTS = 8
CAP = 64
TOKENS = 12288
N_GROUP = 4
N_BLK = 16
N_LOCAL = 8


def level_of(key, extent, shards, low, high):
    def one(axis_at, shards_of):
        heights = jax.random.uniform(jax.random.fold_in(jax.random.fold_in(key, 6), axis_at), (shards_of,), jnp.float32, low / len(shards), high / len(shards))
        return jnp.repeat(jnp.exp(heights), extent[axis_at] // shards_of).reshape((-1,) + (1,) * (len(extent) - axis_at - 1))

    level = one(*shards[0])
    for cut in shards[1:]:
        level = level * one(*cut)
    return level


def deal_out(rng, own, number, rows, amount, top, reach, lean):
    ranking = jax.random.permutation(rng, amount)
    packed, common = shares(amount, rows * top, reach, lean, True), shares(amount, rows * top, reach, lean, False)
    places = jnp.arange(amount)

    def named(sizes, rotation):
        used = int((sizes > 0).sum())
        fixed = max(1, used // 4)
        shifted = fixed + (places - fixed + rotation * (used - fixed)) % max(1, amount - fixed)
        return jnp.zeros((amount,), jnp.int32).at[ranking[jnp.where(places < fixed, places, shifted)]].set(jnp.asarray(sizes, jnp.int32))

    sizes = jnp.where(number % 4 == 0, named(packed, number // 4), named(common, number - number // 4 - 1))
    mixed = jax.random.permutation(jax.random.fold_in(own, 3), amount)
    donor, sink = mixed[0:amount // 2 * 2:2], mixed[1:amount // 2 * 2:2]
    slack = jnp.minimum(sizes[donor] - 1, reach - sizes[sink]) // 2
    slack = jnp.where((donor == ranking[0]) | (sink == ranking[0]) | (sizes[sink] == 0), 0, jnp.maximum(slack, 0))
    shifted = jax.random.randint(jax.random.fold_in(own, 4), (amount // 2,), 0, 1 << 20) % (slack + 1)
    sizes = sizes.at[donor].add(-shifted).at[sink].add(shifted)
    items = jnp.searchsorted(jnp.cumsum(sizes), jnp.arange(rows * top), side="right").astype(jnp.int32)
    grid = items.reshape(top, rows).T
    grid = grid[jax.random.permutation(jax.random.fold_in(own, 1), rows)]
    rotation = jax.random.randint(jax.random.fold_in(own, 2), (rows, 1), 0, top)
    return jnp.take_along_axis(grid, (jnp.arange(top)[None, :] + rotation) % top, axis=1)


def shares(count, total, limit, lean, full):
    weights = [(1 << 20) // math.isqrt(grade ** lean) + 1 for grade in range(1, count + 1)]
    largest = limit if full else min(limit, max(-(-total // count), total * weights[0] // sum(weights)))
    least = 1 if total - largest >= count - 1 else 0
    counts, rest = [largest] + [least] * (count - 1), total - largest - least * (count - 1)
    while rest > 0:
        movable = [i for i in range(1, count) if counts[i] < largest] or [i for i in range(1, count) if counts[i] < limit]
        whole, left = sum([weights[i] for i in movable]), rest
        for i in movable:
            extra = min(limit - counts[i], max(1, left * weights[i] // whole), rest)
            counts[i] = counts[i] + extra
            rest = rest - extra
    return np.array(counts)


def bell_draw(stream_key, shape, width, most, cuts=(), kind=jnp.bfloat16):
    loudness = level_of(stream_key, shape, cuts, -0.22, 0.18) if cuts else 1.0
    result = jax.random.normal(stream_key, shape, jnp.float32) * width * loudness
    return jnp.minimum(jnp.maximum(result, -most), most).astype(kind)


def setup_inputs(seed: int = 0) -> dict:
    keys = jax.random.split(jax.random.key(seed), 8)
    tokens = bell_draw(keys[0], (TOKENS, D), 1.0, 6.0, ((0, 64), (1, 8)))
    d_out = bell_draw(keys[1], (TOKENS, D), 1.0, 6.0, ((0, 64), (1, 8)))
    ids_keys = jax.random.split(jax.random.fold_in(keys[2], 1), TOKENS // TOK_POS)
    ids_turns = jax.random.permutation(jax.random.fold_in(keys[2], 3), TOKENS // TOK_POS)
    ids = jax.vmap(lambda own, number: deal_out(jax.random.fold_in(keys[2], 2), own, number, TOK_POS, EXPERTS, TOP, CAP, 2))(ids_keys, ids_turns).reshape((TOKENS, TOP))
    gates = jnp.clip(0.1 + 0.9 * jax.random.uniform(keys[3], (TOKENS, TOP), jnp.float32) ** level_of(keys[3], (TOKENS, TOP), ((0, 64),), -0.2, 0.2), 0.1, 1.0)
    w_gate = bell_draw(keys[4], (EXPERTS, D, FF), D ** -0.5, 0.125, ((0, 4), (1, 16), (2, 8)))
    w_up = bell_draw(keys[5], (EXPERTS, D, FF), D ** -0.5, 0.125, ((0, 4), (1, 16), (2, 8)))
    w_down = bell_draw(keys[6], (EXPERTS, FF, D), FF ** -0.5, 0.1875, ((0, 4), (1, 8), (2, 16)))
    return {"tokens": tokens, "d_out": d_out, "ids": ids, "gates": gates, "w_gate": w_gate, "w_up": w_up, "w_down": w_down}


def slot_numbers(id_block, experts, capacity):
    flat = id_block.reshape(-1)
    onehot = (flat[:, None] == jnp.arange(experts, dtype=jnp.int32)[None, :]).astype(jnp.int32)
    before = jnp.cumsum(onehot, axis=0) - onehot
    return (flat * capacity + jnp.sum(before * onehot, axis=1)).astype(jnp.int32)


def place_rows(rows, slot_index, total):
    return jnp.zeros((total, rows.shape[1]), rows.dtype).at[slot_index].set(rows)


def rounded(value):
    return lax.optimization_barrier(value.astype(jnp.bfloat16)).astype(jnp.float32)


def expert_pass(operands):
    token_part, grad_part, gate_weight, up_weight, down_weight = operands
    rows = token_part.reshape(-1, D)
    grad_rows = grad_part.reshape(-1, D)
    pre_gate = jnp.dot(rows, gate_weight, preferred_element_type=jnp.float32)
    pre_up = jnp.dot(rows, up_weight, preferred_element_type=jnp.float32)
    squashed = jax.nn.sigmoid(pre_gate)
    hidden = (pre_gate * squashed * pre_up).astype(jnp.bfloat16)
    d_hidden = jnp.dot(grad_rows, down_weight.T, preferred_element_type=jnp.float32)
    d_gate = (d_hidden * pre_up * squashed * (1.0 + pre_gate * (1.0 - squashed))).astype(jnp.bfloat16)
    d_up = (d_hidden * pre_gate * squashed).astype(jnp.bfloat16)
    slice_width = FF // N_LOCAL
    out_rows = jnp.zeros((rows.shape[0], D), jnp.float32)
    input_rows = jnp.zeros((rows.shape[0], D), jnp.float32)
    for part in range(N_LOCAL):
        low = part * slice_width
        high = low + slice_width
        out_rows = out_rows + rounded(jnp.dot(hidden[:, low:high], down_weight[low:high], preferred_element_type=jnp.float32))
        both = jnp.dot(d_gate[:, low:high], gate_weight[:, low:high].T, preferred_element_type=jnp.float32)
        both = both + jnp.dot(d_up[:, low:high], up_weight[:, low:high].T, preferred_element_type=jnp.float32)
        input_rows = input_rows + rounded(both)
    shape_four = (N_GROUP, N_BLK, CAP)
    token_four = rows.reshape(shape_four + (D,)).astype(jnp.float32)
    grad_four = grad_rows.reshape(shape_four + (D,)).astype(jnp.float32)
    hidden_four = hidden.reshape(shape_four + (FF,)).astype(jnp.float32)
    dgate_four = d_gate.reshape(shape_four + (FF,)).astype(jnp.float32)
    dup_four = d_up.reshape(shape_four + (FF,)).astype(jnp.float32)
    grad_gate = jnp.sum(rounded(jnp.einsum("gbcd,gbcf->bdf", token_four, dgate_four)), axis=0)
    grad_up = jnp.sum(rounded(jnp.einsum("gbcd,gbcf->bdf", token_four, dup_four)), axis=0)
    grad_down = jnp.sum(rounded(jnp.einsum("gbcf,gbcd->bfd", hidden_four, grad_four)), axis=0)
    return (out_rows.astype(jnp.bfloat16), input_rows.astype(jnp.bfloat16), grad_gate, grad_up, grad_down)


def reference(tokens, d_out, ids, gates, w_gate, w_up, w_down):
    positions = N_GROUP * N_BLK
    pair_count = TOK_POS * TOP
    token_blocks = tokens.reshape(positions, TOK_POS, D)
    dout_blocks = d_out.reshape(positions, TOK_POS, D)
    gate_blocks = gates.reshape(positions, TOK_POS, TOP)
    slot_index = jax.vmap(lambda block: slot_numbers(block, EXPERTS, CAP))(ids.reshape(positions, TOK_POS, TOP))
    token_pairs = jnp.broadcast_to(token_blocks[:, :, None, :], (positions, TOK_POS, TOP, D)).reshape(positions, pair_count, D)
    grad_pairs = (gate_blocks[:, :, :, None] * dout_blocks[:, :, None, :].astype(jnp.float32)).astype(jnp.bfloat16)
    grad_pairs = grad_pairs.reshape(positions, pair_count, D)
    token_slots = jax.vmap(lambda rows, where: place_rows(rows, where, EXPERTS * CAP))(token_pairs, slot_index)
    grad_slots = jax.vmap(lambda rows, where: place_rows(rows, where, EXPERTS * CAP))(grad_pairs, slot_index)
    token_expert = token_slots.reshape(positions, EXPERTS, CAP, D).transpose(1, 0, 2, 3)
    grad_expert = grad_slots.reshape(positions, EXPERTS, CAP, D).transpose(1, 0, 2, 3)
    out_rows, input_rows, grad_gate, grad_up, grad_down = lax.map(
        expert_pass, (token_expert, grad_expert, w_gate, w_up, w_down))
    out_slots = out_rows.reshape(EXPERTS, positions, CAP, D).transpose(1, 0, 2, 3).reshape(positions, EXPERTS * CAP, D)
    input_slots = input_rows.reshape(EXPERTS, positions, CAP, D).transpose(1, 0, 2, 3).reshape(positions, EXPERTS * CAP, D)
    out_pairs = jax.vmap(lambda rows, where: rows[where])(out_slots, slot_index).reshape(positions, TOK_POS, TOP, D)
    input_pairs = jax.vmap(lambda rows, where: rows[where])(input_slots, slot_index).reshape(positions, TOK_POS, TOP, D)
    moe_out = jnp.sum(gate_blocks[:, :, :, None] * out_pairs.astype(jnp.float32), axis=2).astype(jnp.bfloat16)
    grad_tokens = jnp.sum(input_pairs.astype(jnp.float32), axis=2).astype(jnp.bfloat16)
    grad_gates = jnp.sum(dout_blocks[:, :, None, :].astype(jnp.float32) * out_pairs.astype(jnp.float32), axis=3)
    return (moe_out.reshape(TOKENS, D), grad_tokens.reshape(TOKENS, D), grad_gates.reshape(TOKENS, TOP),
            grad_gate, grad_up, grad_down)
```

```python
import jax
import jax.numpy as jnp
from jax import lax
from jax.sharding import PartitionSpec as P

PLANE = ("group", "local")


def gather_rows(x):
    full = lax.all_gather(x, PLANE, axis=0, tiled=False)
    groups = lax.axis_size("group")
    full = full.reshape(groups, -1, x.shape[0], x.shape[1])
    return jnp.transpose(full, (0, 2, 1, 3)).reshape(groups * x.shape[0], -1)


def scatter_rows(x, rows, cols):
    groups = lax.axis_size("group")
    parts = x.reshape(groups, rows, -1, cols)
    parts = jnp.transpose(parts, (0, 2, 1, 3)).reshape(-1, rows, cols)
    return lax.psum_scatter(parts, PLANE, scatter_dimension=0, tiled=True)[0]


def body(tokens, d_out, ids, gates, w_gate, w_up, w_down):
    f32, bf16 = jnp.float32, jnp.bfloat16
    rows, cols = tokens.shape
    own = w_gate.shape[0]
    toks = gather_rows(tokens)
    douts = gather_rows(d_out)
    all_ids = lax.all_gather(ids, "group", axis=0, tiled=True)
    all_gates = lax.all_gather(gates, "group", axis=0, tiled=True)
    gate_full = lax.all_gather(w_gate, "blk", axis=1, tiled=True)
    up_full = lax.all_gather(w_up, "blk", axis=1, tiled=True)
    down_full = lax.all_gather(w_down, "blk", axis=2, tiled=True)
    mine = lax.axis_index("group") * own + jnp.arange(own, dtype=jnp.int32)
    chosen = all_ids[:, :, None] == mine[None, None, :]
    weight = jnp.sum(jnp.where(chosen, all_gates[:, :, None], 0.0), axis=1)
    routed = jnp.any(chosen, axis=1).astype(f32)
    pre_gate = jnp.einsum("td,edf->tef", toks, gate_full, preferred_element_type=f32)
    pre_up = jnp.einsum("td,edf->tef", toks, up_full, preferred_element_type=f32)
    back = jnp.einsum("td,efd->tef", douts, down_full, preferred_element_type=f32)
    s = jax.nn.sigmoid(pre_gate)
    hidden = pre_gate * s * pre_up
    weighted = (weight[:, :, None] * hidden).astype(bf16)
    d_hidden = weight[:, :, None] * back
    d_gate = (d_hidden * pre_up * s * (1.0 + pre_gate * (1.0 - s))).astype(bf16)
    d_up = (d_hidden * pre_gate * s).astype(bf16)
    pair = jnp.sum(hidden * back, axis=2)
    pair = jnp.sum(jnp.where(chosen, pair[:, None, :], 0.0), axis=2)
    grad_gates = lax.psum(pair, PLANE)
    grad_gates = lax.dynamic_slice_in_dim(grad_gates, lax.axis_index("group") * rows, rows, 0)
    out = jnp.einsum("tef,efd->td", weighted, down_full, preferred_element_type=f32)
    back_in = jnp.einsum("tef,edf->td", d_gate, gate_full, preferred_element_type=f32)
    back_in = back_in + jnp.einsum("tef,edf->td", d_up, up_full, preferred_element_type=f32)
    moe_out = scatter_rows(out.astype(bf16), rows, cols)
    grad_tokens = scatter_rows(back_in.astype(bf16), rows, cols)
    g_gate = jnp.einsum("td,tef->edf", toks, d_gate, preferred_element_type=f32).astype(bf16)
    g_up = jnp.einsum("td,tef->edf", toks, d_up, preferred_element_type=f32).astype(bf16)
    g_down = jnp.einsum("tef,td->efd", weighted, douts, preferred_element_type=f32).astype(bf16)
    g_gate = lax.psum_scatter(g_gate, "blk", scatter_dimension=1, tiled=True)
    g_up = lax.psum_scatter(g_up, "blk", scatter_dimension=1, tiled=True)
    g_down = lax.psum_scatter(g_down, "blk", scatter_dimension=2, tiled=True)
    return (moe_out, grad_tokens, grad_gates, g_gate.astype(f32), g_up.astype(f32), g_down.astype(f32))


def solution(mesh):
    in_specs = (
        P(("group", "blk"), "local"),
        P(("group", "blk"), "local"),
        P(("group", "blk"), None),
        P(("group", "blk"), None),
        P("group", "blk", "local"),
        P("group", "blk", "local"),
        P("group", "local", "blk"),
    )
    out_specs = (
        P(("group", "blk"), "local"),
        P(("group", "blk"), "local"),
        P(("group", "blk"), None),
        P("group", "blk", "local"),
        P("group", "blk", "local"),
        P("group", "local", "blk"),
    )
    return jax.shard_map(body, mesh=mesh, in_specs=in_specs, out_specs=out_specs, check_vma=False)
```

```python
import jax
import jax.numpy as jnp
from jax import lax
from jax.experimental import pallas as pl
from jax.experimental.pallas import tpu as pltpu
from jax.sharding import PartitionSpec as P

F32, BF16 = jnp.float32, jnp.bfloat16
MESH = pl.DeviceIdType.MESH
RX = RY = 4
RZ = 16
ROWS, COLS, HALF = 192, 256, 128
TOK = 768
HID = 768
CHUNK = 384
NSEM = 230


def nt(a, b):
    return lax.dot_general(a, b, (((1,), (1,)), ((), ())), preferred_element_type=F32)


def nn(a, b):
    return jnp.dot(a, b, preferred_element_type=F32)


def side(d):
    return 0 if d == 1 else 1


def gather_chunks(s, d):
    return (0, 1) if s < RZ // 2 else ((0,) if d == 1 else (1,))


def sum_chunks(s, d):
    return (0, 1) if s > 1 else ((0,) if d == 1 else (1,))


def kernel(
    tok_ref, dout_ref, wg_ref, wu_ref, wd_ref, wt_ref,
    moe_ref, gtok_ref, gg_ref, gu_ref, gd_ref, pair_ref,
    tk, wall, acc, dct, am, term, own, zs, zr, ss, sr, op, s1h, r1h, s1f, r1f, op2,
    s2h, r2h, s2f, r2f, wb, wbr, pb, pbr, ssem, rsem,
):
    g, z, l = lax.axis_index("group"), lax.axis_index("blk"), lax.axis_index("local")
    x = lax.div(l, 4) * 2 + lax.div(g, 2)
    y, c = lax.rem(l, 4), lax.rem(g, 2)

    def place(xx, yy, cc, zz):
        return (lax.rem(xx, 2) * 2 + cc, zz, lax.div(xx, 2) * 4 + yy)

    def dev(dx=0, dy=0, dz=0, other=False):
        return place(
            lax.rem(x + dx + RX, RX), lax.rem(y + dy + RY, RY), 1 - c if other else c, lax.rem(z + dz + RZ, RZ)
        )

    sibling = dev(other=True)
    zpos = lambda by: lax.rem(z + by + 2 * RZ, RZ)
    numbers, sent = {}, []

    def number(key):
        return numbers.setdefault(key, len(numbers))

    def put(key, src, dst, to):
        i = number(key)
        made = pltpu.make_async_remote_copy(
            src_ref=src, dst_ref=dst, send_sem=ssem.at[i], recv_sem=rsem.at[i], device_id=to, device_id_type=MESH
        )
        made.start()
        sent.append(made)

    def got(key, dst):
        i = number(key)
        pltpu.make_async_remote_copy(
            src_ref=dst, dst_ref=dst, send_sem=ssem.at[i], recv_sem=rsem.at[i], device_id=sibling, device_id_type=MESH
        ).wait_recv()

    for a in range(2):
        for i in range(16):
            number(("ss", a, i))

    barrier = pltpu.get_barrier_semaphore()
    near = [sibling, dev(dx=1), dev(dx=-1), dev(dx=2), dev(dy=1), dev(dy=-1), dev(dy=2), dev(dz=1), dev(dz=-1)]
    for to in near:
        pl.semaphore_signal(barrier, inc=1, device_id=to, device_id_type=MESH)

    def along(axis, d):
        return dev(dx=d) if axis == 0 else dev(dy=d)

    def rel(a, o1, o2):
        return (o1, o2) if a == 0 else (o2, o1)

    def spot(ox, oy, cc):
        xx, yy = lax.rem(x + ox + RX, RX), lax.rem(y + oy + RY, RY)
        return lax.div(xx, 2) * 4 + yy, pl.multiple_of((lax.rem(xx, 2) * 2 + cc) * ROWS, 64)

    def block(a, o, cc=None):
        ll, row = spot(*o, c if cc is None else cc)
        return tk.at[a, pl.ds(2 * ll, 2), pl.ds(row, ROWS), :]

    def half(a, o, h):
        ll, row = spot(*o, c)
        return tk.at[a, 2 * ll + h, pl.ds(row, ROWS), :]

    row = pl.multiple_of(g * ROWS, 64)
    for e in range(2):
        wall[z, e * 128 : (e + 1) * 128, :] = wg_ref[e].T
        wall[z, 256 + e * 128 : 256 + (e + 1) * 128, :] = wu_ref[e].T
        wall[z, 512 + e * 128 : 512 + (e + 1) * 128, :] = wd_ref[e]
    for a, ref in enumerate((tok_ref, dout_ref)):
        for h in range(2):
            tk[a, 2 * l + h, pl.ds(row, ROWS), :] = ref[:, h * HALF : (h + 1) * HALF]
    wb[0] = wt_ref[...]
    pb[0] = jnp.zeros((8, TOK), F32)
    pl.semaphore_wait(barrier, len(near))

    def wblock(b, ch):
        return wall.at[b, pl.ds(ch * CHUNK, CHUNK), :]

    for ch in range(2):
        for d in (1, -1):
            put(("w", 1, d, ch), wblock(z, ch), wblock(z, ch), dev(dz=d))
    for a in range(2):
        for d in (1, -1):
            put(("g1", a, d), block(a, (0, 0)), block(a, (0, 0)), along(a, d))
    for a in range(2):
        for d in (1, -1):
            put(("g2", a, 0, d), block(a, (0, 0)), block(a, (0, 0)), along(1 - a, d))
    put(("wt", 0), wb.at[0], wbr.at[0], sibling)
    for a in range(2):
        put(("gs", a, 0, 0), block(a, (0, 0)), block(a, (0, 0)), sibling)

    def column(a, o1):
        o = rel(a, o1, 0)
        for d in (1, -1):
            put(("g2", a, o1, d), block(a, o), block(a, o), along(1 - a, d))
        put(("gs", a, o1, 0), block(a, o), block(a, o), sibling)

    def first(a):
        for d in (1, -1):
            o, h = rel(a, -d, 0), side(d)
            got(("g1", a, d), block(a, o))
            put(("g1h", a, d), half(a, o, h), half(a, o, h), along(a, d))
        for d in (1, -1):
            column(a, -d)

    def opposite(a):
        for d in (1, -1):
            got(("g1h", a, d), half(a, rel(a, 2, 0), side(d)))
        column(a, 2)

    def second(a, o1):
        for d in (1, -1):
            o, h = rel(a, o1, -d), side(d)
            got(("g2", a, o1, d), block(a, o))
            put(("g2h", a, o1, d), half(a, o, h), half(a, o, h), along(1 - a, d))
            put(("gs", a, o1, -d), block(a, o), block(a, o), sibling)

    def across(a, o1):
        o = rel(a, o1, 2)
        for d in (1, -1):
            got(("g2h", a, o1, d), half(a, o, side(d)))
        put(("gs", a, o1, 2), block(a, o), block(a, o), sibling)

    def from_sibling(a):
        for o1 in (0, 1, -1, 2):
            for o2 in (0, 1, -1, 2):
                got(("gs", a, o1, o2), block(a, rel(a, o1, o2), 1 - c))

    def weights(s):
        for ch in range(2):
            for d in (1, -1):
                if ch not in gather_chunks(s, d):
                    continue
                where = wblock(zpos(-d * s), ch)
                got(("w", s, d, ch), where)
                if s < RZ // 2 and ch in gather_chunks(s + 1, d):
                    put(("w", s + 1, d, ch), where, where, dev(dz=d))

    def project(b1, b2, fresh=False):
        def tile(t, carry):
            rows = pl.ds(pl.multiple_of(t * 256, 256), 256)
            for a, lo, hi in ((0, 0, 512), (1, 512, 768)):
                lhs = jnp.concatenate([wall[b1, lo:hi, :], wall[b2, lo:hi, :]], axis=1)
                rhs = jnp.concatenate([tk[a, b1, rows, :], tk[a, b2, rows, :]], axis=1)
                value = nt(lhs, rhs)
                acc[t, lo:hi, :] = value if fresh else acc[t, lo:hi, :] + value
            return carry

        lax.fori_loop(0, 3, tile, 0)

    first(0)
    first(1)
    weights(1)
    second(0, 0)
    second(1, 0)
    got(("wt", 0), wbr.at[0])
    wb[1] = wb[0] + wbr[0]
    near_x = place(x + 1 - 2 * lax.rem(x, 2), y, c, z)
    put(("wt", 1), wb.at[1], wbr.at[1], near_x)
    opposite(0)
    opposite(1)
    weights(2)
    for o1 in (-1, 1):
        second(0, o1)
        second(1, o1)
    weights(3)
    for o1 in (0, -1):
        across(0, o1)
        across(1, o1)
    second(0, 2)
    second(1, 2)
    weights(4)
    for o1 in (1, 2):
        across(0, o1)
        across(1, o1)
    got(("wt", 1), wbr.at[1])
    wb[2] = wb[1] + wbr[1]
    from_sibling(0)
    from_sibling(1)
    project(zpos(1), zpos(-1), True)
    project(zpos(2), zpos(-2))
    weights(5)
    project(zpos(3), zpos(-3))
    project(zpos(4), zpos(-4))
    weights(6)
    project(zpos(5), zpos(-5))
    project(zpos(6), zpos(-6))
    weights(7)
    project(zpos(7), zpos(-7))
    weights(8)
    project(z, zpos(8))

    for t in range(3):
        for e in range(2):
            f = slice(e * 128, (e + 1) * 128)
            gate = acc[t, f, :]
            up = acc[t, 256 + e * 128 : 256 + (e + 1) * 128, :]
            back = acc[t, 512 + e * 128 : 512 + (e + 1) * 128, :]
            weight = wb[2, pl.ds(2 * g + e, 1), t * 256 : (t + 1) * 256]
            s = jax.nn.sigmoid(gate)
            hidden = gate * s * up
            d_hidden = weight * back
            dct[t, f, :] = (d_hidden * up * s * (1.0 + gate * (1.0 - s))).astype(BF16)
            dct[t, 256 + e * 128 : 256 + (e + 1) * 128, :] = (d_hidden * gate * s).astype(BF16)
            dct[t, 512 + e * 128 : 512 + (e + 1) * 128, :] = (weight * hidden).astype(BF16)
            pair = jnp.sum(hidden * back, axis=0, keepdims=True)
            pb[0, pl.ds(2 * g + e, 1), t * 256 : (t + 1) * 256] = jnp.where(weight > 0, pair, 0.0)

    def products(b1, b2):
        for a, lo, hi in ((0, 0, 512), (1, 512, 768)):
            total = None
            for t in range(3):
                rhs = jnp.concatenate(
                    [tk[a, b1, t * 256 : (t + 1) * 256, :], tk[a, b2, t * 256 : (t + 1) * 256, :]], axis=1
                )
                value = nn(dct[t, lo:hi, :], rhs)
                total = value if total is None else total + value
            term[lo:hi, :] = total

    def pass_on(s):
        products(zpos(9 - s), z if s == 1 else zpos(s - 9))
        if s == 1:
            own[...] = term[:, 128:]
        for ch in range(2):
            rows = slice(ch * CHUNK, (ch + 1) * CHUNK)
            for d in (1, -1):
                k = side(d)
                if ch not in sum_chunks(s, d):
                    continue
                lanes = slice(0, 128) if s == 1 else slice(k * 128, (k + 1) * 128)
                value = term[rows, lanes]
                if s > 1 and ch in sum_chunks(s - 1, d):
                    got(("r", s - 1, d, ch), zr.at[k, s - 2, rows, :])
                    value = value + zr[k, s - 2, rows, :].astype(F32)
                zs[k, s - 1, rows, :] = value.astype(BF16)
                put(("r", s, d, ch), zs.at[k, s - 1, rows, :], zr.at[k, s - 1, rows, :], dev(dz=d))

    def partials(dx):
        def one(dy, carry):
            i = (dx % 4) * 4 + dy
            xx, yy = lax.rem(x + dx + RX, RX), lax.rem(y + dy, RY)
            ll = lax.div(xx, 2) * 4 + yy
            base = lax.rem(xx, 2) * 2
            mine = pl.multiple_of((base + c) * ROWS, 64)
            theirs = pl.multiple_of((base + 1 - c) * ROWS, 64)
            lhs = jnp.concatenate([am[pl.ds(mine, ROWS), :], am[pl.ds(theirs, ROWS), :]], axis=0)
            for a, lo, hi in ((0, 512, 768), (1, 0, 512)):
                rhs = jnp.concatenate([wall[2 * ll, lo:hi, :], wall[2 * ll + 1, lo:hi, :]], axis=1)
                value = nn(lhs[:, lo:hi], rhs)
                op[a, i] = value[:ROWS]
                ss[a, i] = value[ROWS:].astype(BF16)
                k = a * 16 + i
                pltpu.make_async_remote_copy(
                    src_ref=ss.at[a, i], dst_ref=sr.at[a, i], send_sem=ssem.at[k], recv_sem=rsem.at[k],
                    device_id=sibling, device_id_type=MESH,
                ).start()
            return carry

        lax.fori_loop(0, 4, one, 0)

    def whole(a, o1, o2):
        ox, oy = rel(a, o1, o2)
        i = (ox % 4) * 4 + oy % 4
        got(("ss", a, i), sr.at[a, i])
        return op[a, i] + sr[a, i].astype(F32)

    def far(a, o2):
        value = whole(a, 2, o2).astype(BF16)
        for d in (1, -1):
            k = side(d)
            s1h[a, k, o2] = value[:, k * HALF : (k + 1) * HALF]
            put(("p1h", a, o2, d), s1h.at[a, k, o2], r1h.at[a, k, o2], along(a, d))

    def next_to(a, o2):
        for d in (1, -1):
            k = side(d)
            value = whole(a, d, o2)
            got(("p1h", a, o2, d), r1h.at[a, k, o2])
            more = r1h[a, k, o2].astype(F32)
            for h in range(2):
                part = value[:, h * HALF : (h + 1) * HALF]
                s1f[a, k, o2, :, h * HALF : (h + 1) * HALF] = (part + more if h == k else part).astype(BF16)
            put(("p1f", a, o2, d), s1f.at[a, k, o2], r1f.at[a, k, o2], along(a, d))

    def here(a, o2):
        value = whole(a, 0, o2)
        for d in (1, -1):
            got(("p1f", a, o2, d), r1f.at[a, side(d), o2])
            value = value + r1f[a, side(d), o2].astype(F32)
        op2[a, o2] = value
        if o2 == 2:
            low = value.astype(BF16)
            for d in (1, -1):
                k = side(d)
                s2h[a, k] = low[:, k * HALF : (k + 1) * HALF]
                put(("p2h", a, d), s2h.at[a, k], r2h.at[a, k], along(1 - a, d))

    def turn(a):
        for d in (1, -1):
            k = side(d)
            got(("p2h", a, d), r2h.at[a, k])
            more = r2h[a, k].astype(F32)
            for h in range(2):
                part = op2[a, d % 4, :, h * HALF : (h + 1) * HALF]
                s2f[a, k, :, h * HALF : (h + 1) * HALF] = (part + more if h == k else part).astype(BF16)
            put(("p2f", a, d), s2f.at[a, k], r2f.at[a, k], along(1 - a, d))

    def finish(a, ref):
        value = op2[a, 0]
        for d in (1, -1):
            got(("p2f", a, d), r2f.at[a, side(d)])
            value = value + r2f[a, side(d)].astype(F32)
        ref[...] = value.astype(BF16)

    partner = [
        sibling, near_x, dev(dx=2), place(x, y + 1 - 2 * lax.rem(y, 2), c, z), dev(dy=2),
    ]

    def share(k):
        if k:
            got(("p", k - 1), pbr.at[k - 1])
            pb[k] = pb[k - 1] + pbr[k - 1]
        if k < len(partner):
            put(("p", k), pb.at[k], pbr.at[k], partner[k])
        else:
            pair_ref[...] = pb[k]

    pass_on(1)
    share(0)
    for t in range(3):
        for u in range(6):
            am[t * 256 : (t + 1) * 256, u * 128 : (u + 1) * 128] = dct[t, u * 128 : (u + 1) * 128, :].T
    pass_on(2)
    partials(2)
    share(1)
    pass_on(3)
    partials(1)
    partials(-1)
    share(2)
    partials(0)
    pass_on(4)
    for o2 in (2, 1, 3, 0):
        for a in range(2):
            far(a, o2)
    share(3)
    pass_on(5)
    for o2 in (2, 1, 3, 0):
        for a in range(2):
            next_to(a, o2)
    share(4)
    pass_on(6)
    for o2 in (2, 1, 3):
        for a in range(2):
            here(a, o2)
    share(5)
    pass_on(7)
    for a in range(2):
        here(a, 0)
        turn(a)
    pass_on(8)
    finish(0, moe_ref)
    finish(1, gtok_ref)
    for ch in range(2):
        for d in (1, -1):
            got(("r", 8, d, ch), zr.at[side(d), 7, pl.ds(ch * CHUNK, CHUNK), :])
    for e in range(2):
        for base, ref in ((0, gg_ref), (256, gu_ref), (512, gd_ref)):
            rows = slice(base + e * 128, base + (e + 1) * 128)
            value = own[rows, :] + zr[0, 7, rows, :].astype(F32) + zr[1, 7, rows, :].astype(F32)
            ref[e] = value if base == 512 else value.T

    for made in sent:
        made.wait_send()
    for a in range(2):
        for i in range(16):
            k = a * 16 + i
            pltpu.make_async_remote_copy(
                src_ref=ss.at[a, i], dst_ref=sr.at[a, i], send_sem=ssem.at[k], recv_sem=rsem.at[k],
                device_id=sibling, device_id_type=MESH,
            ).wait_send()
    assert len(numbers) <= NSEM, len(numbers)


def body(tokens, d_out, ids, gates, w_gate, w_up, w_down):
    experts = w_gate.shape[0] * lax.axis_size("group")
    place = lax.axis_index("group") * ROWS
    chosen = ids.T[:, None, :] == jnp.arange(experts, dtype=jnp.int32)[None, :, None]
    weight = jnp.sum(jnp.where(chosen, gates.T[:, None, :], 0.0), axis=0)
    weight = lax.dynamic_update_slice(jnp.zeros((experts, TOK), F32), weight, (0, place))
    vm = pl.BlockSpec(memory_space=pltpu.VMEM)
    shape = jax.ShapeDtypeStruct
    moe, gtok, gg, gu, gd, pair = pl.pallas_call(
        kernel,
        out_shape=(
            shape(tokens.shape, BF16),
            shape(tokens.shape, BF16),
            shape(w_gate.shape, F32),
            shape(w_up.shape, F32),
            shape(w_down.shape, F32),
            shape((experts, TOK), F32),
        ),
        in_specs=[vm] * 6,
        out_specs=(vm,) * 6,
        scratch_shapes=[
            pltpu.VMEM((2, 16, TOK, 128), BF16),
            pltpu.VMEM((16, HID, 128), BF16),
            pltpu.VMEM((3, HID, 256), F32),
            pltpu.VMEM((3, HID, 256), BF16),
            pltpu.VMEM((TOK, HID), BF16),
            pltpu.VMEM((HID, 256), F32),
            pltpu.VMEM((HID, 128), F32),
            pltpu.VMEM((2, 8, HID, 128), BF16),
            pltpu.VMEM((2, 8, HID, 128), BF16),
            pltpu.VMEM((2, 16, ROWS, COLS), BF16),
            pltpu.VMEM((2, 16, ROWS, COLS), BF16),
            pltpu.VMEM((2, 16, ROWS, COLS), F32),
            pltpu.VMEM((2, 2, 4, ROWS, HALF), BF16),
            pltpu.VMEM((2, 2, 4, ROWS, HALF), BF16),
            pltpu.VMEM((2, 2, 4, ROWS, COLS), BF16),
            pltpu.VMEM((2, 2, 4, ROWS, COLS), BF16),
            pltpu.VMEM((2, 4, ROWS, COLS), F32),
            pltpu.VMEM((2, 2, ROWS, HALF), BF16),
            pltpu.VMEM((2, 2, ROWS, HALF), BF16),
            pltpu.VMEM((2, 2, ROWS, COLS), BF16),
            pltpu.VMEM((2, 2, ROWS, COLS), BF16),
            pltpu.VMEM((3, 8, TOK), F32),
            pltpu.VMEM((2, 8, TOK), F32),
            pltpu.VMEM((6, 8, TOK), F32),
            pltpu.VMEM((5, 8, TOK), F32),
            pltpu.SemaphoreType.DMA((NSEM,)),
            pltpu.SemaphoreType.DMA((NSEM,)),
        ],
        compiler_params=pltpu.CompilerParams(
            collective_id=0, has_side_effects=True, vmem_limit_bytes=58 * 2**20
        ),
    )(tokens, d_out, w_gate, w_up, w_down, weight)
    pair = lax.dynamic_slice(pair, (0, place), (experts, ROWS))
    grad_gates = jnp.sum(jnp.where(chosen, pair[None, :, :], 0.0), axis=1).T
    return (moe, gtok, grad_gates, gg, gu, gd)


def solution(mesh):
    in_specs = (
        P(("group", "blk"), "local"),
        P(("group", "blk"), "local"),
        P(("group", "blk"), None),
        P(("group", "blk"), None),
        P("group", "blk", "local"),
        P("group", "blk", "local"),
        P("group", "local", "blk"),
    )
    out_specs = (
        P(("group", "blk"), "local"),
        P(("group", "blk"), "local"),
        P(("group", "blk"), None),
        P("group", "blk", "local"),
        P("group", "blk", "local"),
        P("group", "local", "blk"),
    )
    return jax.shard_map(body, mesh=mesh, in_specs=in_specs, out_specs=out_specs, check_vma=False)
```

```python
import jax
import jax.numpy as jnp
from jax import lax
from jax.experimental import pallas as pl
from jax.experimental.pallas import tpu as pltpu
from jax.sharding import PartitionSpec as P

F32, BF16 = jnp.float32, jnp.bfloat16
MESH = pl.DeviceIdType.MESH
RX = RY = 4
RZ = 16
ROWS, COLS, HALF = 192, 256, 128
TOK = 768
HID = 768
CHUNK = 192
CHUNKS = 4
NSEM = 280


def nt(a, b):
    return lax.dot_general(a, b, (((1,), (1,)), ((), ())), preferred_element_type=F32)


def nn(a, b):
    return jnp.dot(a, b, preferred_element_type=F32)


def side(d):
    return 0 if d == 1 else 1


def gather_chunks(s, d):
    return (0, 1, 2, 3) if s < RZ // 2 else ((0, 1) if d == 1 else (2, 3))


def sum_chunks(s, d):
    return (0, 1, 2, 3) if s > 1 else ((0, 1) if d == 1 else (2, 3))


def kernel(
    tok_ref, dout_ref, wg_ref, wu_ref, wd_ref, ids_ref, gates_ref,
    moe_ref, gtok_ref, gg_ref, gu_ref, gd_ref, pair_ref,
    tk, wall, acc, dct, am, term, own, zs, zr, ss, sr, op, s1h, r1h, s1f, r1f, op2,
    s2h, r2h, s2f, r2f, wb, wbr, pb, pbr, ssem, rsem,
):
    g, z, l = lax.axis_index("group"), lax.axis_index("blk"), lax.axis_index("local")
    x = lax.div(l, 4) * 2 + lax.div(g, 2)
    y, c = lax.rem(l, 4), lax.rem(g, 2)

    def place(xx, yy, cc, zz):
        return (lax.rem(xx, 2) * 2 + cc, zz, lax.div(xx, 2) * 4 + yy)

    def dev(dx=0, dy=0, dz=0, other=False):
        return place(
            lax.rem(x + dx + RX, RX), lax.rem(y + dy + RY, RY), 1 - c if other else c, lax.rem(z + dz + RZ, RZ)
        )

    sibling = dev(other=True)
    zpos = lambda by: lax.rem(z + by + 2 * RZ, RZ)
    numbers, sent = {}, []

    def number(key):
        return numbers.setdefault(key, len(numbers))

    def put(key, src, dst, to):
        i = number(key)
        made = pltpu.make_async_remote_copy(
            src_ref=src, dst_ref=dst, send_sem=ssem.at[i], recv_sem=rsem.at[i], device_id=to, device_id_type=MESH
        )
        made.start()
        sent.append(made)

    def got(key, dst):
        i = number(key)
        pltpu.make_async_remote_copy(
            src_ref=dst, dst_ref=dst, send_sem=ssem.at[i], recv_sem=rsem.at[i], device_id=sibling, device_id_type=MESH
        ).wait_recv()

    for a in range(2):
        for i in range(16):
            number(("ss", a, i))

    barrier = pltpu.get_barrier_semaphore()
    near = [sibling, dev(dx=1), dev(dx=-1), dev(dx=2), dev(dy=1), dev(dy=-1), dev(dy=2), dev(dz=1), dev(dz=-1)]
    for to in near:
        pl.semaphore_signal(barrier, inc=1, device_id=to, device_id_type=MESH)

    def along(axis, d):
        return dev(dx=d) if axis == 0 else dev(dy=d)

    def rel(a, o1, o2):
        return (o1, o2) if a == 0 else (o2, o1)

    def spot(ox, oy, cc):
        xx, yy = lax.rem(x + ox + RX, RX), lax.rem(y + oy + RY, RY)
        return lax.div(xx, 2) * 4 + yy, pl.multiple_of((lax.rem(xx, 2) * 2 + cc) * ROWS, 64)

    def block(a, o, cc=None):
        ll, row = spot(*o, c if cc is None else cc)
        return tk.at[a, pl.ds(2 * ll, 2), pl.ds(row, ROWS), :]

    def half(a, o, h):
        ll, row = spot(*o, c)
        return tk.at[a, 2 * ll + h, pl.ds(row, ROWS), :]

    row = pl.multiple_of(g * ROWS, 64)
    for e in range(2):
        wall[z, e * 128 : (e + 1) * 128, :] = wg_ref[e].T
        wall[z, 256 + e * 128 : 256 + (e + 1) * 128, :] = wu_ref[e].T
        wall[z, 512 + e * 128 : 512 + (e + 1) * 128, :] = wd_ref[e]
    for a, ref in enumerate((tok_ref, dout_ref)):
        for h in range(2):
            tk[a, 2 * l + h, pl.ds(row, ROWS), :] = ref[:, h * HALF : (h + 1) * HALF]
    number_of = lax.broadcasted_iota(jnp.int32, (8, ROWS), 0)
    picked = [ids_ref[k : k + 1, :] == number_of for k in range(2)]
    weights_of = jnp.where(picked[0], gates_ref[0:1, :], 0.0) + jnp.where(picked[1], gates_ref[1:2, :], 0.0)
    for q in range(4):
        wb[0, :, q * ROWS : (q + 1) * ROWS] = jnp.where(g == q, weights_of, 0.0)
    pb[0] = jnp.zeros((8, TOK), F32)
    pl.semaphore_wait(barrier, len(near))

    def wblock(b, ch):
        return wall.at[b, pl.ds(ch * CHUNK, CHUNK), :]

    for ch in range(CHUNKS):
        for d in (1, -1):
            put(("w", 1, d, ch), wblock(z, ch), wblock(z, ch), dev(dz=d))
    for a in range(2):
        for d in (1, -1):
            put(("g1", a, d), block(a, (0, 0)), block(a, (0, 0)), along(a, d))
    for a in range(2):
        for d in (1, -1):
            put(("g2", a, 0, d), block(a, (0, 0)), block(a, (0, 0)), along(1 - a, d))
    put(("wt", 0), wb.at[0], wbr.at[0], sibling)
    for a in range(2):
        put(("gs", a, 0, 0), block(a, (0, 0)), block(a, (0, 0)), sibling)

    def column(a, o1):
        o = rel(a, o1, 0)
        for d in (1, -1):
            put(("g2", a, o1, d), block(a, o), block(a, o), along(1 - a, d))
        put(("gs", a, o1, 0), block(a, o), block(a, o), sibling)

    def first(a):
        for d in (1, -1):
            o, h = rel(a, -d, 0), side(d)
            got(("g1", a, d), block(a, o))
            put(("g1h", a, d), half(a, o, h), half(a, o, h), along(a, d))
        for d in (1, -1):
            column(a, -d)

    def opposite(a):
        for d in (1, -1):
            got(("g1h", a, d), half(a, rel(a, 2, 0), side(d)))
        column(a, 2)

    def second(a, o1):
        for d in (1, -1):
            o, h = rel(a, o1, -d), side(d)
            got(("g2", a, o1, d), block(a, o))
            put(("g2h", a, o1, d), half(a, o, h), half(a, o, h), along(1 - a, d))
            put(("gs", a, o1, -d), block(a, o), block(a, o), sibling)

    def across(a, o1):
        o = rel(a, o1, 2)
        for d in (1, -1):
            got(("g2h", a, o1, d), half(a, o, side(d)))
        put(("gs", a, o1, 2), block(a, o), block(a, o), sibling)

    def from_sibling(a):
        for o1 in (0, 1, -1, 2):
            for o2 in (0, 1, -1, 2):
                got(("gs", a, o1, o2), block(a, rel(a, o1, o2), 1 - c))

    def weights(s):
        for ch in range(CHUNKS):
            for d in (1, -1):
                if ch not in gather_chunks(s, d):
                    continue
                where = wblock(zpos(-d * s), ch)
                got(("w", s, d, ch), where)
                if s < RZ // 2 and ch in gather_chunks(s + 1, d):
                    put(("w", s + 1, d, ch), where, where, dev(dz=d))

    def project(b1, b2, fresh=False):
        def tile(t, carry):
            rows = pl.ds(pl.multiple_of(t * 256, 256), 256)
            for a, lo, hi in ((0, 0, 512), (1, 512, 768)):
                lhs = jnp.concatenate([wall[b1, lo:hi, :], wall[b2, lo:hi, :]], axis=1)
                rhs = jnp.concatenate([tk[a, b1, rows, :], tk[a, b2, rows, :]], axis=1)
                value = nt(lhs, rhs)
                acc[t, lo:hi, :] = value if fresh else acc[t, lo:hi, :] + value
            return carry

        lax.fori_loop(0, 3, tile, 0)

    first(0)
    first(1)
    weights(1)
    second(0, 0)
    second(1, 0)
    got(("wt", 0), wbr.at[0])
    wb[1] = wb[0] + wbr[0]
    near_x = place(x + 1 - 2 * lax.rem(x, 2), y, c, z)
    put(("wt", 1), wb.at[1], wbr.at[1], near_x)
    opposite(0)
    opposite(1)
    weights(2)
    for o1 in (-1, 1):
        second(0, o1)
        second(1, o1)
    weights(3)
    for o1 in (0, -1):
        across(0, o1)
        across(1, o1)
    second(0, 2)
    second(1, 2)
    weights(4)
    for o1 in (1, 2):
        across(0, o1)
        across(1, o1)
    got(("wt", 1), wbr.at[1])
    wb[2] = wb[1] + wbr[1]
    from_sibling(0)
    from_sibling(1)
    project(zpos(1), zpos(-1), True)
    project(zpos(2), zpos(-2))
    weights(5)
    project(zpos(3), zpos(-3))
    project(zpos(4), zpos(-4))
    weights(6)
    project(zpos(5), zpos(-5))
    project(zpos(6), zpos(-6))
    weights(7)
    project(zpos(7), zpos(-7))
    weights(8)
    project(z, zpos(8))

    for t in range(3):
        for e in range(2):
            f = slice(e * 128, (e + 1) * 128)
            gate = acc[t, f, :]
            up = acc[t, 256 + e * 128 : 256 + (e + 1) * 128, :]
            back = acc[t, 512 + e * 128 : 512 + (e + 1) * 128, :]
            weight = wb[2, pl.ds(2 * g + e, 1), t * 256 : (t + 1) * 256]
            s = jax.nn.sigmoid(gate)
            hidden = gate * s * up
            d_hidden = weight * back
            dct[t, f, :] = (d_hidden * up * s * (1.0 + gate * (1.0 - s))).astype(BF16)
            dct[t, 256 + e * 128 : 256 + (e + 1) * 128, :] = (d_hidden * gate * s).astype(BF16)
            dct[t, 512 + e * 128 : 512 + (e + 1) * 128, :] = (weight * hidden).astype(BF16)
            pair = jnp.sum(hidden * back, axis=0, keepdims=True)
            pb[0, pl.ds(2 * g + e, 1), t * 256 : (t + 1) * 256] = jnp.where(weight > 0, pair, 0.0)

    def products(b1, b2):
        for a, lo, hi in ((0, 0, 512), (1, 512, 768)):
            total = None
            for t in range(3):
                rhs = jnp.concatenate(
                    [tk[a, b1, t * 256 : (t + 1) * 256, :], tk[a, b2, t * 256 : (t + 1) * 256, :]], axis=1
                )
                value = nn(dct[t, lo:hi, :], rhs)
                total = value if total is None else total + value
            term[lo:hi, :] = total

    def pass_on(s):
        products(zpos(9 - s), z if s == 1 else zpos(s - 9))
        if s == 1:
            own[...] = term[:, 128:]
        for ch in range(CHUNKS):
            rows = slice(ch * CHUNK, (ch + 1) * CHUNK)
            for d in (1, -1):
                k = side(d)
                if ch not in sum_chunks(s, d):
                    continue
                lanes = slice(0, 128) if s == 1 else slice(k * 128, (k + 1) * 128)
                value = term[rows, lanes]
                if s > 1 and ch in sum_chunks(s - 1, d):
                    got(("r", s - 1, d, ch), zr.at[k, s - 2, rows, :])
                    value = value + zr[k, s - 2, rows, :].astype(F32)
                zs[k, s - 1, rows, :] = value.astype(BF16)
                put(("r", s, d, ch), zs.at[k, s - 1, rows, :], zr.at[k, s - 1, rows, :], dev(dz=d))

    def partials(dx):
        def one(dy, carry):
            i = (dx % 4) * 4 + dy
            xx, yy = lax.rem(x + dx + RX, RX), lax.rem(y + dy, RY)
            ll = lax.div(xx, 2) * 4 + yy
            base = lax.rem(xx, 2) * 2
            mine = pl.multiple_of((base + c) * ROWS, 64)
            theirs = pl.multiple_of((base + 1 - c) * ROWS, 64)
            lhs = jnp.concatenate([am[pl.ds(mine, ROWS), :], am[pl.ds(theirs, ROWS), :]], axis=0)
            for a, lo, hi in ((0, 512, 768), (1, 0, 512)):
                rhs = jnp.concatenate([wall[2 * ll, lo:hi, :], wall[2 * ll + 1, lo:hi, :]], axis=1)
                value = nn(lhs[:, lo:hi], rhs)
                op[a, i] = value[:ROWS]
                ss[a, i] = value[ROWS:].astype(BF16)
                k = a * 16 + i
                pltpu.make_async_remote_copy(
                    src_ref=ss.at[a, i], dst_ref=sr.at[a, i], send_sem=ssem.at[k], recv_sem=rsem.at[k],
                    device_id=sibling, device_id_type=MESH,
                ).start()
            return carry

        lax.fori_loop(0, 4, one, 0)

    def whole(a, o1, o2):
        ox, oy = rel(a, o1, o2)
        i = (ox % 4) * 4 + oy % 4
        got(("ss", a, i), sr.at[a, i])
        return op[a, i] + sr[a, i].astype(F32)

    def far(a, o2):
        value = whole(a, 2, o2).astype(BF16)
        for d in (1, -1):
            k = side(d)
            s1h[a, k, o2] = value[:, k * HALF : (k + 1) * HALF]
            put(("p1h", a, o2, d), s1h.at[a, k, o2], r1h.at[a, k, o2], along(a, d))

    def next_to(a, o2):
        for d in (1, -1):
            k = side(d)
            value = whole(a, d, o2)
            got(("p1h", a, o2, d), r1h.at[a, k, o2])
            more = r1h[a, k, o2].astype(F32)
            for h in range(2):
                part = value[:, h * HALF : (h + 1) * HALF]
                s1f[a, k, o2, :, h * HALF : (h + 1) * HALF] = (part + more if h == k else part).astype(BF16)
            put(("p1f", a, o2, d), s1f.at[a, k, o2], r1f.at[a, k, o2], along(a, d))

    def here(a, o2):
        value = whole(a, 0, o2)
        for d in (1, -1):
            got(("p1f", a, o2, d), r1f.at[a, side(d), o2])
            value = value + r1f[a, side(d), o2].astype(F32)
        op2[a, o2] = value
        if o2 == 2:
            low = value.astype(BF16)
            for d in (1, -1):
                k = side(d)
                s2h[a, k] = low[:, k * HALF : (k + 1) * HALF]
                put(("p2h", a, d), s2h.at[a, k], r2h.at[a, k], along(1 - a, d))

    def turn(a):
        for d in (1, -1):
            k = side(d)
            got(("p2h", a, d), r2h.at[a, k])
            more = r2h[a, k].astype(F32)
            for h in range(2):
                part = op2[a, d % 4, :, h * HALF : (h + 1) * HALF]
                s2f[a, k, :, h * HALF : (h + 1) * HALF] = (part + more if h == k else part).astype(BF16)
            put(("p2f", a, d), s2f.at[a, k], r2f.at[a, k], along(1 - a, d))

    def finish(a, ref):
        value = op2[a, 0]
        for d in (1, -1):
            got(("p2f", a, d), r2f.at[a, side(d)])
            value = value + r2f[a, side(d)].astype(F32)
        ref[...] = value.astype(BF16)

    partner = [
        sibling, near_x, dev(dx=2), place(x, y + 1 - 2 * lax.rem(y, 2), c, z), dev(dy=2),
    ]

    def share(k):
        if k:
            got(("p", k - 1), pbr.at[k - 1])
            pb[k] = pb[k - 1] + pbr[k - 1]
        if k < len(partner):
            put(("p", k), pb.at[k], pbr.at[k], partner[k])
        else:
            mine = jnp.zeros((8, ROWS), F32)
            for q in range(4):
                mine = jnp.where(g == q, pb[k, :, q * ROWS : (q + 1) * ROWS], mine)
            for j in range(2):
                pair_ref[j : j + 1, :] = jnp.sum(jnp.where(picked[j], mine, 0.0), axis=0, keepdims=True)

    pass_on(1)
    share(0)
    for t in range(3):
        for u in range(6):
            am[t * 256 : (t + 1) * 256, u * 128 : (u + 1) * 128] = dct[t, u * 128 : (u + 1) * 128, :].T
    pass_on(2)
    partials(2)
    share(1)
    pass_on(3)
    partials(1)
    partials(-1)
    share(2)
    partials(0)
    pass_on(4)
    for o2 in (2, 1, 3, 0):
        for a in range(2):
            far(a, o2)
    share(3)
    pass_on(5)
    for o2 in (2, 1, 3, 0):
        for a in range(2):
            next_to(a, o2)
    share(4)
    pass_on(6)
    for o2 in (2, 1, 3):
        for a in range(2):
            here(a, o2)
    share(5)
    pass_on(7)
    for a in range(2):
        here(a, 0)
        turn(a)
    pass_on(8)
    finish(0, moe_ref)
    finish(1, gtok_ref)
    for ch in range(CHUNKS):
        for d in (1, -1):
            got(("r", 8, d, ch), zr.at[side(d), 7, pl.ds(ch * CHUNK, CHUNK), :])
    for e in range(2):
        for base, ref in ((0, gg_ref), (256, gu_ref), (512, gd_ref)):
            rows = slice(base + e * 128, base + (e + 1) * 128)
            value = own[rows, :] + zr[0, 7, rows, :].astype(F32) + zr[1, 7, rows, :].astype(F32)
            ref[e] = value if base == 512 else value.T

    for made in sent:
        made.wait_send()
    for a in range(2):
        for i in range(16):
            k = a * 16 + i
            pltpu.make_async_remote_copy(
                src_ref=ss.at[a, i], dst_ref=sr.at[a, i], send_sem=ssem.at[k], recv_sem=rsem.at[k],
                device_id=sibling, device_id_type=MESH,
            ).wait_send()
    assert len(numbers) <= NSEM, len(numbers)


def hand_over(*refs):
    for src, dst in zip(refs[:6], refs[6:]):
        dst[...] = src[...]


def body(tokens, d_out, ids, gates, w_gate, w_up, w_down):
    vm = pl.BlockSpec(memory_space=pltpu.VMEM)
    shape = jax.ShapeDtypeStruct
    moe, gtok, gg, gu, gd, pair = pl.pallas_call(
        kernel,
        out_shape=(
            shape(tokens.shape, BF16),
            shape(tokens.shape, BF16),
            shape(w_gate.shape, F32),
            shape(w_up.shape, F32),
            shape(w_down.shape, F32),
            shape(gates.shape[::-1], F32),
        ),
        in_specs=[vm] * 7,
        out_specs=(vm,) * 6,
        scratch_shapes=[
            pltpu.VMEM((2, 16, TOK, 128), BF16),
            pltpu.VMEM((16, HID, 128), BF16),
            pltpu.VMEM((3, HID, 256), F32),
            pltpu.VMEM((3, HID, 256), BF16),
            pltpu.VMEM((TOK, HID), BF16),
            pltpu.VMEM((HID, 256), F32),
            pltpu.VMEM((HID, 128), F32),
            pltpu.VMEM((2, 8, HID, 128), BF16),
            pltpu.VMEM((2, 8, HID, 128), BF16),
            pltpu.VMEM((2, 16, ROWS, COLS), BF16),
            pltpu.VMEM((2, 16, ROWS, COLS), BF16),
            pltpu.VMEM((2, 16, ROWS, COLS), F32),
            pltpu.VMEM((2, 2, 4, ROWS, HALF), BF16),
            pltpu.VMEM((2, 2, 4, ROWS, HALF), BF16),
            pltpu.VMEM((2, 2, 4, ROWS, COLS), BF16),
            pltpu.VMEM((2, 2, 4, ROWS, COLS), BF16),
            pltpu.VMEM((2, 4, ROWS, COLS), F32),
            pltpu.VMEM((2, 2, ROWS, HALF), BF16),
            pltpu.VMEM((2, 2, ROWS, HALF), BF16),
            pltpu.VMEM((2, 2, ROWS, COLS), BF16),
            pltpu.VMEM((2, 2, ROWS, COLS), BF16),
            pltpu.VMEM((3, 8, TOK), F32),
            pltpu.VMEM((2, 8, TOK), F32),
            pltpu.VMEM((6, 8, TOK), F32),
            pltpu.VMEM((5, 8, TOK), F32),
            pltpu.SemaphoreType.DMA((NSEM,)),
            pltpu.SemaphoreType.DMA((NSEM,)),
        ],
        compiler_params=pltpu.CompilerParams(
            collective_id=0, has_side_effects=True, vmem_limit_bytes=58 * 2**20
        ),
    )(tokens, d_out, w_gate, w_up, w_down, ids.T, gates.T)
    made = (moe, gtok, gg, gu, gd, pair)
    moe, gtok, gg, gu, gd, pair = pl.pallas_call(
        hand_over,
        out_shape=tuple(shape(a.shape, a.dtype) for a in made),
        in_specs=[vm] * 6,
        out_specs=(vm,) * 6,
        compiler_params=pltpu.CompilerParams(vmem_limit_bytes=58 * 2**20),
    )(*made)
    return (moe, gtok, pair.T, gg, gu, gd)


def solution(mesh):
    in_specs = (
        P(("group", "blk"), "local"),
        P(("group", "blk"), "local"),
        P(("group", "blk"), None),
        P(("group", "blk"), None),
        P("group", "blk", "local"),
        P("group", "blk", "local"),
        P("group", "local", "blk"),
    )
    out_specs = (
        P(("group", "blk"), "local"),
        P(("group", "blk"), "local"),
        P(("group", "blk"), None),
        P("group", "blk", "local"),
        P("group", "blk", "local"),
        P("group", "local", "blk"),
    )
    return jax.shard_map(body, mesh=mesh, in_specs=in_specs, out_specs=out_specs, check_vma=False)
```

```python
import jax
import jax.numpy as jnp
from jax import lax
from jax.experimental import pallas as pl
from jax.experimental.pallas import tpu as pltpu
from jax.sharding import PartitionSpec as P

F32, BF16 = jnp.float32, jnp.bfloat16
MESH = pl.DeviceIdType.MESH
RX = RY = 4
RZ = 16
ROWS, COLS, HALF = 192, 256, 128
TOK = 768
HID = 768
CHUNK = 192
EXP = 384
NSEM = 280


def nt(a, b):
    return lax.dot_general(a, b, (((1,), (1,)), ((), ())), preferred_element_type=F32)


def nn(a, b):
    return jnp.dot(a, b, preferred_element_type=F32)


def side(d):
    return 0 if d == 1 else 1


def gather_chunks(s, d):
    return (0, 1) if s < RZ // 2 else ((0,) if d == 1 else (1,))


def sum_chunks(s, d):
    return (0, 1) if s > 1 else ((0,) if d == 1 else (1,))


def kernel(
    tok_ref, dout_ref, wg_ref, wu_ref, wd_ref, ids_ref, gates_ref,
    moe_ref, gtok_ref, gg_ref, gu_ref, gd_ref, pair_ref,
    tk, wall, acc, dct, am, term, own, zs, zr, ss, sr, op, s1h, r1h, s1f, r1f, op2,
    s2h, r2h, s2f, r2f, wb, wbr, pb, pbr, ssem, rsem,
):
    g, z, l = lax.axis_index("group"), lax.axis_index("blk"), lax.axis_index("local")
    x = lax.div(l, 4) * 2 + lax.div(g, 2)
    y, c = lax.rem(l, 4), lax.rem(g, 2)

    def place(xx, yy, cc, zz):
        return (lax.rem(xx, 2) * 2 + cc, zz, lax.div(xx, 2) * 4 + yy)

    def dev(dx=0, dy=0, dz=0, other=False):
        return place(
            lax.rem(x + dx + RX, RX), lax.rem(y + dy + RY, RY), 1 - c if other else c, lax.rem(z + dz + RZ, RZ)
        )

    sibling = dev(other=True)
    zpos = lambda by: lax.rem(z + by + 2 * RZ, RZ)
    numbers, sent = {}, []

    def number(key):
        return numbers.setdefault(key, len(numbers))

    def put(key, src, dst, to):
        i = number(key)
        made = pltpu.make_async_remote_copy(
            src_ref=src, dst_ref=dst, send_sem=ssem.at[i], recv_sem=rsem.at[i], device_id=to, device_id_type=MESH
        )
        made.start()
        sent.append(made)

    def got(key, dst):
        i = number(key)
        pltpu.make_async_remote_copy(
            src_ref=dst, dst_ref=dst, send_sem=ssem.at[i], recv_sem=rsem.at[i], device_id=sibling, device_id_type=MESH
        ).wait_recv()

    barrier = pltpu.get_barrier_semaphore()
    near = [sibling, dev(dx=1), dev(dx=-1), dev(dx=2), dev(dy=1), dev(dy=-1), dev(dy=2), dev(dz=1), dev(dz=-1)]
    for to in near:
        pl.semaphore_signal(barrier, inc=1, device_id=to, device_id_type=MESH)

    def along(axis, d):
        return dev(dx=d) if axis == 0 else dev(dy=d)

    def rel(a, o1, o2):
        return (o1, o2) if a == 0 else (o2, o1)

    def spot(ox, oy, cc):
        xx, yy = lax.rem(x + ox + RX, RX), lax.rem(y + oy + RY, RY)
        return lax.div(xx, 2) * 4 + yy, pl.multiple_of((lax.rem(xx, 2) * 2 + cc) * ROWS, 64)

    def block(a, o, cc=None):
        ll, row = spot(*o, c if cc is None else cc)
        return tk.at[a, pl.ds(2 * ll, 2), pl.ds(row, ROWS), :]

    def half(a, o, h):
        ll, row = spot(*o, c)
        return tk.at[a, 2 * ll + h, pl.ds(row, ROWS), :]

    row = pl.multiple_of(g * ROWS, 64)
    for e in range(2):
        wall[z, e * EXP : e * EXP + 128, :] = wg_ref[e].T
        wall[z, e * EXP + 128 : e * EXP + 256, :] = wu_ref[e].T
        wall[z, e * EXP + 256 : (e + 1) * EXP, :] = wd_ref[e]
    for a, ref in enumerate((tok_ref, dout_ref)):
        for h in range(2):
            tk[a, 2 * l + h, pl.ds(row, ROWS), :] = ref[:, h * HALF : (h + 1) * HALF]
    number_of = lax.broadcasted_iota(jnp.int32, (8, ROWS), 0)
    picked = [ids_ref[k : k + 1, :] == number_of for k in range(2)]
    weights_of = jnp.where(picked[0], gates_ref[0:1, :], 0.0) + jnp.where(picked[1], gates_ref[1:2, :], 0.0)
    for q in range(4):
        wb[0, :, q * ROWS : (q + 1) * ROWS] = jnp.where(g == q, weights_of, 0.0)
    pb[0] = jnp.zeros((8, TOK), F32)
    pl.semaphore_wait(barrier, len(near))

    def wblock(b, e, ch):
        return wall.at[b, pl.ds(e * EXP + ch * CHUNK, CHUNK), :]

    def start_weights(e):
        for ch in range(2):
            for d in (1, -1):
                put(("w", e, 1, d, ch), wblock(z, e, ch), wblock(z, e, ch), dev(dz=d))

    start_weights(0)
    start_weights(1)
    for a in range(2):
        for d in (1, -1):
            put(("g1", a, d), block(a, (0, 0)), block(a, (0, 0)), along(a, d))
    for a in range(2):
        for d in (1, -1):
            put(("g2", a, 0, d), block(a, (0, 0)), block(a, (0, 0)), along(1 - a, d))
    put(("wt", 0), wb.at[0], wbr.at[0], sibling)
    for a in range(2):
        put(("gs", a, 0, 0), block(a, (0, 0)), block(a, (0, 0)), sibling)

    def column(a, o1):
        o = rel(a, o1, 0)
        for d in (1, -1):
            put(("g2", a, o1, d), block(a, o), block(a, o), along(1 - a, d))
        put(("gs", a, o1, 0), block(a, o), block(a, o), sibling)

    def first(a):
        for d in (1, -1):
            o, h = rel(a, -d, 0), side(d)
            got(("g1", a, d), block(a, o))
            put(("g1h", a, d), half(a, o, h), half(a, o, h), along(a, d))
        for d in (1, -1):
            column(a, -d)

    def opposite(a):
        for d in (1, -1):
            got(("g1h", a, d), half(a, rel(a, 2, 0), side(d)))
        column(a, 2)

    def second(a, o1):
        for d in (1, -1):
            o, h = rel(a, o1, -d), side(d)
            got(("g2", a, o1, d), block(a, o))
            put(("g2h", a, o1, d), half(a, o, h), half(a, o, h), along(1 - a, d))
            put(("gs", a, o1, -d), block(a, o), block(a, o), sibling)

    def across(a, o1):
        o = rel(a, o1, 2)
        for d in (1, -1):
            got(("g2h", a, o1, d), half(a, o, side(d)))
        put(("gs", a, o1, 2), block(a, o), block(a, o), sibling)

    def from_sibling(a):
        for o1 in (0, 1, -1, 2):
            for o2 in (0, 1, -1, 2):
                got(("gs", a, o1, o2), block(a, rel(a, o1, o2), 1 - c))

    def weights(e, s):
        for ch in range(2):
            for d in (1, -1):
                if ch not in gather_chunks(s, d):
                    continue
                where = wblock(zpos(-d * s), e, ch)
                got(("w", e, s, d, ch), where)
                if s < RZ // 2 and ch in gather_chunks(s + 1, d):
                    put(("w", e, s + 1, d, ch), where, where, dev(dz=d))

    def project(e, steps, fresh=False):
        pairs = [(z, zpos(8)) if s == 8 else (zpos(s), zpos(-s)) for s in steps]

        def tile(t, carry):
            rows = pl.ds(pl.multiple_of(t * 256, 256), 256)
            for a, lo, hi in ((0, e * EXP, e * EXP + 256), (1, e * EXP + 256, (e + 1) * EXP)):
                total = None if fresh else acc[t, lo:hi, :]
                for b1, b2 in pairs:
                    lhs = jnp.concatenate([wall[b1, lo:hi, :], wall[b2, lo:hi, :]], axis=1)
                    rhs = jnp.concatenate([tk[a, b1, rows, :], tk[a, b2, rows, :]], axis=1)
                    value = nt(lhs, rhs)
                    total = value if total is None else total + value
                acc[t, lo:hi, :] = total
            return carry

        lax.fori_loop(0, 3, tile, 0)

    def middle(e):
        f = [slice(e * EXP + i * 128, e * EXP + (i + 1) * 128) for i in range(3)]
        for t in range(3):
            gate, up, back = (acc[t, i, :] for i in f)
            weight = wb[2, pl.ds(2 * g + e, 1), t * 256 : (t + 1) * 256]
            s = jax.nn.sigmoid(gate)
            hidden = gate * s * up
            d_hidden = weight * back
            dct[t, f[0], :] = (d_hidden * up * s * (1.0 + gate * (1.0 - s))).astype(BF16)
            dct[t, f[1], :] = (d_hidden * gate * s).astype(BF16)
            dct[t, f[2], :] = (weight * hidden).astype(BF16)
            pair = jnp.sum(hidden * back, axis=0, keepdims=True)
            pb[0, pl.ds(2 * g + e, 1), t * 256 : (t + 1) * 256] = jnp.where(weight > 0, pair, 0.0)

    def products(e, b1, b2):
        for a, lo, hi in ((0, 0, 256), (1, 256, EXP)):
            total = None
            for t in range(3):
                rhs = jnp.concatenate(
                    [tk[a, b1, t * 256 : (t + 1) * 256, :], tk[a, b2, t * 256 : (t + 1) * 256, :]], axis=1
                )
                value = nn(dct[t, e * EXP + lo : e * EXP + hi, :], rhs)
                total = value if total is None else total + value
            term[lo:hi, :] = total

    def pass_on(e, s):
        products(e, zpos(9 - s), z if s == 1 else zpos(s - 9))
        if s == 1:
            own[e * EXP : (e + 1) * EXP, :] = term[:, 128:]
        for ch in range(2):
            rows = slice(e * EXP + ch * CHUNK, e * EXP + (ch + 1) * CHUNK)
            for d in (1, -1):
                k = side(d)
                if ch not in sum_chunks(s, d):
                    continue
                lanes = slice(0, 128) if s == 1 else slice(k * 128, (k + 1) * 128)
                value = term[ch * CHUNK : (ch + 1) * CHUNK, lanes]
                if s > 1 and ch in sum_chunks(s - 1, d):
                    got(("r", e, s - 1, d, ch), zr.at[k, s - 2, rows, :])
                    value = value + zr[k, s - 2, rows, :].astype(F32)
                zs[k, s - 1, rows, :] = value.astype(BF16)
                put(("r", e, s, d, ch), zs.at[k, s - 1, rows, :], zr.at[k, s - 1, rows, :], dev(dz=d))

    def partial(a, o1, o2):
        i = (o1 % 4) * 4 + o2 if a == 0 else o2 * 4 + o1 % 4
        dx, dy = (o1, o2) if a == 0 else (o2, o1)
        xx, yy = lax.rem(x + dx + RX, RX), lax.rem(y + dy + RY, RY)
        ll = lax.div(xx, 2) * 4 + yy
        base = lax.rem(xx, 2) * 2
        mine = pl.ds(pl.multiple_of((base + c) * ROWS, 64), ROWS)
        theirs = pl.ds(pl.multiple_of((base + 1 - c) * ROWS, 64), ROWS)
        lo, hi = (256, EXP) if a == 0 else (0, 256)
        cols = [slice(e * EXP + lo, e * EXP + hi) for e in range(2)]
        lhs = jnp.concatenate([jnp.concatenate([am[r, k] for k in cols], axis=1) for r in (mine, theirs)], axis=0)
        rhs = jnp.concatenate(
            [jnp.concatenate([wall[2 * ll + h, k, :] for k in cols], axis=0) for h in range(2)], axis=1
        )
        value = nn(lhs, rhs)
        op[a, i] = value[:ROWS]
        ss[a, i] = value[ROWS:].astype(BF16)
        put(("ss", a, i), ss.at[a, i], sr.at[a, i], sibling)

    def whole(a, o1, o2):
        ox, oy = rel(a, o1, o2)
        i = (ox % 4) * 4 + oy % 4
        got(("ss", a, i), sr.at[a, i])
        return op[a, i] + sr[a, i].astype(F32)

    def far(a, o2):
        value = whole(a, 2, o2).astype(BF16)
        for d in (1, -1):
            k = side(d)
            s1h[a, k, o2] = value[:, k * HALF : (k + 1) * HALF]
            put(("p1h", a, o2, d), s1h.at[a, k, o2], r1h.at[a, k, o2], along(a, d))

    def next_to(a, o2):
        for d in (1, -1):
            k = side(d)
            value = whole(a, d, o2)
            got(("p1h", a, o2, d), r1h.at[a, k, o2])
            more = r1h[a, k, o2].astype(F32)
            for h in range(2):
                part = value[:, h * HALF : (h + 1) * HALF]
                s1f[a, k, o2, :, h * HALF : (h + 1) * HALF] = (part + more if h == k else part).astype(BF16)
            put(("p1f", a, o2, d), s1f.at[a, k, o2], r1f.at[a, k, o2], along(a, d))

    def here(a, o2):
        value = whole(a, 0, o2)
        for d in (1, -1):
            got(("p1f", a, o2, d), r1f.at[a, side(d), o2])
            value = value + r1f[a, side(d), o2].astype(F32)
        op2[a, o2] = value
        if o2 == 2:
            low = value.astype(BF16)
            for d in (1, -1):
                k = side(d)
                s2h[a, k] = low[:, k * HALF : (k + 1) * HALF]
                put(("p2h", a, d), s2h.at[a, k], r2h.at[a, k], along(1 - a, d))

    def turn(a):
        for d in (1, -1):
            k = side(d)
            got(("p2h", a, d), r2h.at[a, k])
            more = r2h[a, k].astype(F32)
            for h in range(2):
                part = op2[a, d % 4, :, h * HALF : (h + 1) * HALF]
                s2f[a, k, :, h * HALF : (h + 1) * HALF] = (part + more if h == k else part).astype(BF16)
            put(("p2f", a, d), s2f.at[a, k], r2f.at[a, k], along(1 - a, d))

    def finish(a, ref):
        value = op2[a, 0]
        for d in (1, -1):
            got(("p2f", a, d), r2f.at[a, side(d)])
            value = value + r2f[a, side(d)].astype(F32)
        ref[...] = value.astype(BF16)

    near_x = place(x + 1 - 2 * lax.rem(x, 2), y, c, z)
    partner = [
        sibling, near_x, dev(dx=2), place(x, y + 1 - 2 * lax.rem(y, 2), c, z), dev(dy=2),
    ]

    def share(k):
        if k:
            got(("p", k - 1), pbr.at[k - 1])
            pb[k] = pb[k - 1] + pbr[k - 1]
        if k < len(partner):
            put(("p", k), pb.at[k], pbr.at[k], partner[k])
        else:
            mine = jnp.zeros((8, ROWS), F32)
            for q in range(4):
                mine = jnp.where(g == q, pb[k, :, q * ROWS : (q + 1) * ROWS], mine)
            for j in range(2):
                pair_ref[j : j + 1, :] = jnp.sum(jnp.where(picked[j], mine, 0.0), axis=0, keepdims=True)

    def each(what, *orders):
        for o in orders:
            for a in range(2):
                what(a, o)

    def partials(a, o1):
        for o2 in (2, 1, 3, 0):
            partial(a, o1, o2)

    def turned(t):
        for u in range(6):
            am[t * 256 : (t + 1) * 256, u * 128 : (u + 1) * 128] = dct[t, u * 128 : (u + 1) * 128, :].T

    first(0)
    first(1)
    weights(0, 1)
    each(second, 0)
    got(("wt", 0), wbr.at[0])
    wb[1] = wb[0] + wbr[0]
    put(("wt", 1), wb.at[1], wbr.at[1], near_x)
    weights(1, 1)
    opposite(0)
    opposite(1)
    weights(0, 2)
    each(second, -1)
    weights(1, 2)
    each(second, 1)
    weights(0, 3)
    each(across, 0)
    weights(1, 3)
    each(second, 2)
    each(across, -1)
    weights(0, 4)
    each(across, 1)
    weights(1, 4)
    each(across, 2)
    weights(0, 5)
    got(("wt", 1), wbr.at[1])
    wb[2] = wb[1] + wbr[1]
    from_sibling(0)
    from_sibling(1)
    weights(1, 5)
    project(0, (1, 2, 3), True)
    weights(0, 6)
    project(1, (1, 2, 3), True)
    weights(1, 6)
    project(0, (4, 5, 6))
    weights(0, 7)
    project(1, (4, 5, 6))
    weights(1, 7)
    project(0, (7,))
    weights(0, 8)
    project(0, (8,))
    middle(0)
    pass_on(0, 1)
    weights(1, 8)
    project(1, (7, 8))
    middle(1)
    pass_on(1, 1)
    share(0)
    turned(0)
    turned(1)
    turned(2)
    pass_on(0, 2)
    each(partials, 2)
    pass_on(1, 2)
    each(far, 2, 1)
    partials(0, 1)
    pass_on(0, 3)
    each(far, 3, 0)
    partials(1, 1)
    pass_on(1, 3)
    share(1)
    partials(0, -1)
    pass_on(0, 4)
    partials(1, -1)
    pass_on(1, 4)
    each(next_to, 2, 1)
    pass_on(0, 5)
    each(next_to, 3, 0)
    share(2)
    pass_on(1, 5)
    partials(0, 0)
    pass_on(0, 6)
    partials(1, 0)
    each(here, 2)
    pass_on(1, 6)
    each(here, 1, 3)
    share(3)
    pass_on(0, 7)
    each(here, 0)
    pass_on(1, 7)
    turn(0)
    turn(1)
    share(4)
    pass_on(0, 8)
    share(5)
    pass_on(1, 8)
    finish(0, moe_ref)
    finish(1, gtok_ref)
    for e in range(2):
        for ch in range(2):
            for d in (1, -1):
                got(("r", e, 8, d, ch), zr.at[side(d), 7, pl.ds(e * EXP + ch * CHUNK, CHUNK), :])
    for e in range(2):
        for base, ref in ((0, gg_ref), (128, gu_ref), (256, gd_ref)):
            rows = slice(e * EXP + base, e * EXP + base + 128)
            value = own[rows, :] + zr[0, 7, rows, :].astype(F32) + zr[1, 7, rows, :].astype(F32)
            ref[e] = value if base == 256 else value.T

    for made in sent:
        made.wait_send()
    assert len(numbers) <= NSEM, len(numbers)


def hand_over(*refs):
    for src, dst in zip(refs[:6], refs[6:]):
        dst[...] = src[...]


def body(tokens, d_out, ids, gates, w_gate, w_up, w_down):
    vm = pl.BlockSpec(memory_space=pltpu.VMEM)
    shape = jax.ShapeDtypeStruct
    moe, gtok, gg, gu, gd, pair = pl.pallas_call(
        kernel,
        out_shape=(
            shape(tokens.shape, BF16),
            shape(tokens.shape, BF16),
            shape(w_gate.shape, F32),
            shape(w_up.shape, F32),
            shape(w_down.shape, F32),
            shape(gates.shape[::-1], F32),
        ),
        in_specs=[vm] * 7,
        out_specs=(vm,) * 6,
        scratch_shapes=[
            pltpu.VMEM((2, 16, TOK, 128), BF16),
            pltpu.VMEM((16, HID, 128), BF16),
            pltpu.VMEM((3, HID, 256), F32),
            pltpu.VMEM((3, HID, 256), BF16),
            pltpu.VMEM((TOK, HID), BF16),
            pltpu.VMEM((EXP, 256), F32),
            pltpu.VMEM((HID, 128), F32),
            pltpu.VMEM((2, 8, HID, 128), BF16),
            pltpu.VMEM((2, 8, HID, 128), BF16),
            pltpu.VMEM((2, 16, ROWS, COLS), BF16),
            pltpu.VMEM((2, 16, ROWS, COLS), BF16),
            pltpu.VMEM((2, 16, ROWS, COLS), F32),
            pltpu.VMEM((2, 2, 4, ROWS, HALF), BF16),
            pltpu.VMEM((2, 2, 4, ROWS, HALF), BF16),
            pltpu.VMEM((2, 2, 4, ROWS, COLS), BF16),
            pltpu.VMEM((2, 2, 4, ROWS, COLS), BF16),
            pltpu.VMEM((2, 4, ROWS, COLS), F32),
            pltpu.VMEM((2, 2, ROWS, HALF), BF16),
            pltpu.VMEM((2, 2, ROWS, HALF), BF16),
            pltpu.VMEM((2, 2, ROWS, COLS), BF16),
            pltpu.VMEM((2, 2, ROWS, COLS), BF16),
            pltpu.VMEM((3, 8, TOK), F32),
            pltpu.VMEM((2, 8, TOK), F32),
            pltpu.VMEM((6, 8, TOK), F32),
            pltpu.VMEM((5, 8, TOK), F32),
            pltpu.SemaphoreType.DMA((NSEM,)),
            pltpu.SemaphoreType.DMA((NSEM,)),
        ],
        compiler_params=pltpu.CompilerParams(
            collective_id=0, has_side_effects=True, vmem_limit_bytes=58 * 2**20
        ),
    )(tokens, d_out, w_gate, w_up, w_down, ids.T, gates.T)
    made = (moe, gtok, gg, gu, gd, pair)
    moe, gtok, gg, gu, gd, pair = pl.pallas_call(
        hand_over,
        out_shape=tuple(shape(a.shape, a.dtype) for a in made),
        in_specs=[vm] * 6,
        out_specs=(vm,) * 6,
        compiler_params=pltpu.CompilerParams(vmem_limit_bytes=58 * 2**20),
    )(*made)
    return (moe, gtok, pair.T, gg, gu, gd)


def solution(mesh):
    in_specs = (
        P(("group", "blk"), "local"),
        P(("group", "blk"), "local"),
        P(("group", "blk"), None),
        P(("group", "blk"), None),
        P("group", "blk", "local"),
        P("group", "blk", "local"),
        P("group", "local", "blk"),
    )
    out_specs = (
        P(("group", "blk"), "local"),
        P(("group", "blk"), "local"),
        P(("group", "blk"), None),
        P("group", "blk", "local"),
        P("group", "blk", "local"),
        P("group", "local", "blk"),
    )
    return jax.shard_map(body, mesh=mesh, in_specs=in_specs, out_specs=out_specs, check_vma=False)
```

```python
import jax
import jax.numpy as jnp
from jax import lax
from jax.experimental import pallas as pl
from jax.experimental.pallas import tpu as pltpu
from jax.sharding import PartitionSpec as P

F32, BF16 = jnp.float32, jnp.bfloat16
MESH = pl.DeviceIdType.MESH
RX = RY = 4
RZ = 16
ROWS, COLS, HALF = 192, 256, 128
TOK = 768
HID = 768
CHUNK = 192
EXP = 384
NSEM = 280


def nt(a, b):
    return lax.dot_general(a, b, (((1,), (1,)), ((), ())), preferred_element_type=F32)


def nn(a, b):
    return jnp.dot(a, b, preferred_element_type=F32)


def side(d):
    return 0 if d == 1 else 1


def gather_chunks(s, d):
    return (0, 1) if s < RZ // 2 else ((0,) if d == 1 else (1,))


def sum_chunks(s, d):
    return (0, 1) if s > 1 else ((0,) if d == 1 else (1,))


def kernel(
    tok_ref, dout_ref, wg_ref, wu_ref, wd_ref, ids_ref, gates_ref,
    moe_ref, gtok_ref, gg_ref, gu_ref, gd_ref, pair_ref,
    tk, wall, acc, dct, am, term, own, zs, zr, ss, sr, op, s1h, r1h, s1f, r1f, op2,
    s2h, r2h, s2f, r2f, wb, wbr, pb, pbr, wtmp, ids_in, gates_in, rows_out, grads_out, pair_out,
    ssem, rsem, isem, osem,
):
    g, z, l = lax.axis_index("group"), lax.axis_index("blk"), lax.axis_index("local")
    x = lax.div(l, 4) * 2 + lax.div(g, 2)
    y, c = lax.rem(l, 4), lax.rem(g, 2)

    def place(xx, yy, cc, zz):
        return (lax.rem(xx, 2) * 2 + cc, zz, lax.div(xx, 2) * 4 + yy)

    def dev(dx=0, dy=0, dz=0, other=False):
        return place(
            lax.rem(x + dx + RX, RX), lax.rem(y + dy + RY, RY), 1 - c if other else c, lax.rem(z + dz + RZ, RZ)
        )

    sibling = dev(other=True)
    zpos = lambda by: lax.rem(z + by + 2 * RZ, RZ)
    numbers, sent = {}, []

    def number(key):
        return numbers.setdefault(key, len(numbers))

    def put(key, src, dst, to):
        i = number(key)
        made = pltpu.make_async_remote_copy(
            src_ref=src, dst_ref=dst, send_sem=ssem.at[i], recv_sem=rsem.at[i], device_id=to, device_id_type=MESH
        )
        made.start()
        sent.append(made)

    def got(key, dst):
        i = number(key)
        pltpu.make_async_remote_copy(
            src_ref=dst, dst_ref=dst, send_sem=ssem.at[i], recv_sem=rsem.at[i], device_id=sibling, device_id_type=MESH
        ).wait_recv()

    for a in range(2):
        for i in range(16):
            number(("ss", a, i))

    barrier = pltpu.get_barrier_semaphore()
    near = [sibling, dev(dx=1), dev(dx=-1), dev(dx=2), dev(dy=1), dev(dy=-1), dev(dy=2), dev(dz=1), dev(dz=-1)]
    for to in near:
        pl.semaphore_signal(barrier, inc=1, device_id=to, device_id_type=MESH)

    def along(axis, d):
        return dev(dx=d) if axis == 0 else dev(dy=d)

    def rel(a, o1, o2):
        return (o1, o2) if a == 0 else (o2, o1)

    def spot(ox, oy, cc):
        xx, yy = lax.rem(x + ox + RX, RX), lax.rem(y + oy + RY, RY)
        return lax.div(xx, 2) * 4 + yy, pl.multiple_of((lax.rem(xx, 2) * 2 + cc) * ROWS, 64)

    def block(a, o, cc=None):
        ll, row = spot(*o, c if cc is None else cc)
        return tk.at[a, pl.ds(2 * ll, 2), pl.ds(row, ROWS), :]

    def half(a, o, h):
        ll, row = spot(*o, c)
        return tk.at[a, 2 * ll + h, pl.ds(row, ROWS), :]

    row = pl.multiple_of(g * ROWS, 64)
    fetched, leaving = [], []

    def leave(src, dst):
        made = pltpu.make_async_copy(src, dst, osem.at[len(leaving)])
        made.start()
        leaving.append(made)

    def fetch(src, dst):
        made = pltpu.make_async_copy(src, dst, isem.at[len(fetched)])
        made.start()
        fetched.append(made)

    fetch(wg_ref, wtmp.at[0])
    fetch(wu_ref, wtmp.at[1])
    for e in range(2):
        fetch(wd_ref.at[e], wall.at[z, pl.ds(e * EXP + 256, 128), :])
    fetch(ids_ref, ids_in)
    fetch(gates_ref, gates_in)
    for a, ref in enumerate((tok_ref, dout_ref)):
        for h in range(2):
            fetch(ref.at[:, pl.ds(h * HALF, HALF)], tk.at[a, 2 * l + h, pl.ds(row, ROWS), :])
    for made in fetched:
        made.wait()
    for e in range(2):
        wall[z, e * EXP : e * EXP + 128, :] = wtmp[0, e].T
        wall[z, e * EXP + 128 : e * EXP + 256, :] = wtmp[1, e].T
    number_of = lax.broadcasted_iota(jnp.int32, (8, ROWS), 0)
    picked = [ids_in[k : k + 1, :] == number_of for k in range(2)]
    weights_of = jnp.where(picked[0], gates_in[0:1, :], 0.0) + jnp.where(picked[1], gates_in[1:2, :], 0.0)
    for q in range(4):
        wb[0, :, q * ROWS : (q + 1) * ROWS] = jnp.where(g == q, weights_of, 0.0)
    pb[0] = jnp.zeros((8, TOK), F32)
    pl.semaphore_wait(barrier, len(near))

    def wblock(b, e, ch):
        return wall.at[b, pl.ds(e * EXP + ch * CHUNK, CHUNK), :]

    def start_weights(e):
        for ch in range(2):
            for d in (1, -1):
                put(("w", e, 1, d, ch), wblock(z, e, ch), wblock(z, e, ch), dev(dz=d))

    start_weights(0)
    start_weights(1)
    for a in range(2):
        for d in (1, -1):
            put(("g1", a, d), block(a, (0, 0)), block(a, (0, 0)), along(a, d))
    for a in range(2):
        for d in (1, -1):
            put(("g2", a, 0, d), block(a, (0, 0)), block(a, (0, 0)), along(1 - a, d))
    put(("wt", 0), wb.at[0], wbr.at[0], sibling)
    for a in range(2):
        put(("gs", a, 0, 0), block(a, (0, 0)), block(a, (0, 0)), sibling)

    def column(a, o1):
        o = rel(a, o1, 0)
        for d in (1, -1):
            put(("g2", a, o1, d), block(a, o), block(a, o), along(1 - a, d))
        put(("gs", a, o1, 0), block(a, o), block(a, o), sibling)

    def first(a):
        for d in (1, -1):
            o, h = rel(a, -d, 0), side(d)
            got(("g1", a, d), block(a, o))
            put(("g1h", a, d), half(a, o, h), half(a, o, h), along(a, d))
        for d in (1, -1):
            column(a, -d)

    def opposite(a):
        for d in (1, -1):
            got(("g1h", a, d), half(a, rel(a, 2, 0), side(d)))
        column(a, 2)

    def second(a, o1):
        for d in (1, -1):
            o, h = rel(a, o1, -d), side(d)
            got(("g2", a, o1, d), block(a, o))
            put(("g2h", a, o1, d), half(a, o, h), half(a, o, h), along(1 - a, d))
            put(("gs", a, o1, -d), block(a, o), block(a, o), sibling)

    def across(a, o1):
        o = rel(a, o1, 2)
        for d in (1, -1):
            got(("g2h", a, o1, d), half(a, o, side(d)))
        put(("gs", a, o1, 2), block(a, o), block(a, o), sibling)

    def from_sibling(a):
        for o1 in (0, 1, -1, 2):
            for o2 in (0, 1, -1, 2):
                got(("gs", a, o1, o2), block(a, rel(a, o1, o2), 1 - c))

    def weights(e, s):
        for ch in range(2):
            for d in (1, -1):
                if ch not in gather_chunks(s, d):
                    continue
                where = wblock(zpos(-d * s), e, ch)
                got(("w", e, s, d, ch), where)
                if s < RZ // 2 and ch in gather_chunks(s + 1, d):
                    put(("w", e, s + 1, d, ch), where, where, dev(dz=d))

    def project(e, steps, fresh=False):
        pairs = [(z, zpos(8)) if s == 8 else (zpos(s), zpos(-s)) for s in steps]

        def tile(t, carry):
            rows = pl.ds(pl.multiple_of(t * 256, 256), 256)
            for a, lo, hi in ((0, e * EXP, e * EXP + 256), (1, e * EXP + 256, (e + 1) * EXP)):
                total = None if fresh else acc[t, lo:hi, :]
                for b1, b2 in pairs:
                    lhs = jnp.concatenate([wall[b1, lo:hi, :], wall[b2, lo:hi, :]], axis=1)
                    rhs = jnp.concatenate([tk[a, b1, rows, :], tk[a, b2, rows, :]], axis=1)
                    value = nt(lhs, rhs)
                    total = value if total is None else total + value
                acc[t, lo:hi, :] = total
            return carry

        lax.fori_loop(0, 3, tile, 0)

    def middle(e):
        f = [slice(e * EXP + i * 128, e * EXP + (i + 1) * 128) for i in range(3)]
        for t in range(3):
            gate, up, back = (acc[t, i, :] for i in f)
            weight = wb[2, pl.ds(2 * g + e, 1), t * 256 : (t + 1) * 256]
            s = jax.nn.sigmoid(gate)
            hidden = gate * s * up
            d_hidden = weight * back
            dct[t, f[0], :] = (d_hidden * up * s * (1.0 + gate * (1.0 - s))).astype(BF16)
            dct[t, f[1], :] = (d_hidden * gate * s).astype(BF16)
            dct[t, f[2], :] = (weight * hidden).astype(BF16)
            pair = jnp.sum(hidden * back, axis=0, keepdims=True)
            pb[0, pl.ds(2 * g + e, 1), t * 256 : (t + 1) * 256] = jnp.where(weight > 0, pair, 0.0)

    def products(e, b1, b2):
        for a, lo, hi in ((0, 0, 256), (1, 256, EXP)):
            total = None
            for t in range(3):
                rhs = jnp.concatenate(
                    [tk[a, b1, t * 256 : (t + 1) * 256, :], tk[a, b2, t * 256 : (t + 1) * 256, :]], axis=1
                )
                value = nn(dct[t, e * EXP + lo : e * EXP + hi, :], rhs)
                total = value if total is None else total + value
            term[e, lo:hi, :] = total

    def begin(e, s):
        products(e, zpos(9 - s), z if s == 1 else zpos(s - 9))
        if s == 1:
            own[e * EXP : (e + 1) * EXP, :] = term[e, :, 128:]
        for d in (1, -1):
            for ch in sum_chunks(s, d):
                if s == 1 or ch not in sum_chunks(s - 1, d):
                    step(e, s, d, ch, False)

    def step(e, s, d, ch, more):
        k = side(d)
        rows = slice(e * EXP + ch * CHUNK, e * EXP + (ch + 1) * CHUNK)
        lanes = slice(0, 128) if s == 1 else slice(k * 128, (k + 1) * 128)
        value = term[e, ch * CHUNK : (ch + 1) * CHUNK, lanes]
        if more:
            got(("r", e, s - 1, d, ch), zr.at[k, s - 2, rows, :])
            value = value + zr[k, s - 2, rows, :].astype(F32)
        zs[k, s - 1, rows, :] = value.astype(BF16)
        put(("r", e, s, d, ch), zs.at[k, s - 1, rows, :], zr.at[k, s - 1, rows, :], dev(dz=d))

    def pass_on(e, s):
        if s > 2:
            begin(e, s)
        for ch in range(2):
            for d in (1, -1):
                if ch in sum_chunks(s - 1, d):
                    step(e, s, d, ch, True)

    def handed(a, i):
        k = a * 16 + i
        return pltpu.make_async_remote_copy(
            src_ref=ss.at[a, i], dst_ref=sr.at[a, i], send_sem=ssem.at[k], recv_sem=rsem.at[k],
            device_id=sibling, device_id_type=MESH,
        )

    def partial(a, o1, o2):
        i = (o1 % 4) * 4 + o2 if a == 0 else o2 * 4 + o1 % 4
        dx, dy = (o1, o2) if a == 0 else (o2, o1)
        xx, yy = lax.rem(x + dx + RX, RX), lax.rem(y + dy + RY, RY)
        ll = lax.div(xx, 2) * 4 + yy
        base = lax.rem(xx, 2) * 2
        mine = pl.ds(pl.multiple_of((base + c) * ROWS, 64), ROWS)
        theirs = pl.ds(pl.multiple_of((base + 1 - c) * ROWS, 64), ROWS)
        lo, hi = (256, EXP) if a == 0 else (0, 256)
        cols = [slice(e * EXP + lo, e * EXP + hi) for e in range(2)]
        lhs = jnp.concatenate([jnp.concatenate([am[r, k] for k in cols], axis=1) for r in (mine, theirs)], axis=0)
        rhs = jnp.concatenate(
            [jnp.concatenate([wall[2 * ll + h, k, :] for k in cols], axis=0) for h in range(2)], axis=1
        )
        value = nn(lhs, rhs)
        op[a, i] = value[:ROWS]
        ss[a, i] = value[ROWS:].astype(BF16)
        handed(a, i).start()

    def whole(a, o1, o2):
        ox, oy = rel(a, o1, o2)
        i = (ox % 4) * 4 + oy % 4
        got(("ss", a, i), sr.at[a, i])
        return op[a, i] + sr[a, i].astype(F32)

    def far(a, o2):
        value = whole(a, 2, o2).astype(BF16)
        for d in (1, -1):
            k = side(d)
            s1h[a, k, o2] = value[:, k * HALF : (k + 1) * HALF]
            put(("p1h", a, o2, d), s1h.at[a, k, o2], r1h.at[a, k, o2], along(a, d))

    def next_to(a, o2):
        for d in (1, -1):
            k = side(d)
            value = whole(a, d, o2)
            got(("p1h", a, o2, d), r1h.at[a, k, o2])
            more = r1h[a, k, o2].astype(F32)
            for h in range(2):
                part = value[:, h * HALF : (h + 1) * HALF]
                s1f[a, k, o2, :, h * HALF : (h + 1) * HALF] = (part + more if h == k else part).astype(BF16)
            put(("p1f", a, o2, d), s1f.at[a, k, o2], r1f.at[a, k, o2], along(a, d))

    def here(a, o2):
        value = whole(a, 0, o2)
        for d in (1, -1):
            got(("p1f", a, o2, d), r1f.at[a, side(d), o2])
            value = value + r1f[a, side(d), o2].astype(F32)
        op2[a, o2] = value
        if o2 == 2:
            low = value.astype(BF16)
            for d in (1, -1):
                k = side(d)
                s2h[a, k] = low[:, k * HALF : (k + 1) * HALF]
                put(("p2h", a, d), s2h.at[a, k], r2h.at[a, k], along(1 - a, d))

    def turn(a):
        for d in (1, -1):
            k = side(d)
            got(("p2h", a, d), r2h.at[a, k])
            more = r2h[a, k].astype(F32)
            for h in range(2):
                part = op2[a, d % 4, :, h * HALF : (h + 1) * HALF]
                s2f[a, k, :, h * HALF : (h + 1) * HALF] = (part + more if h == k else part).astype(BF16)
            put(("p2f", a, d), s2f.at[a, k], r2f.at[a, k], along(1 - a, d))

    def finish(a, ref):
        value = op2[a, 0]
        for d in (1, -1):
            got(("p2f", a, d), r2f.at[a, side(d)])
            value = value + r2f[a, side(d)].astype(F32)
        rows_out[a] = value.astype(BF16)
        leave(rows_out.at[a], ref)

    near_x = place(x + 1 - 2 * lax.rem(x, 2), y, c, z)
    partner = [
        sibling, near_x, dev(dx=2), place(x, y + 1 - 2 * lax.rem(y, 2), c, z), dev(dy=2),
    ]

    def share(k):
        if k:
            got(("p", k - 1), pbr.at[k - 1])
            pb[k] = pb[k - 1] + pbr[k - 1]
        if k < len(partner):
            put(("p", k), pb.at[k], pbr.at[k], partner[k])
        else:
            mine = jnp.zeros((8, ROWS), F32)
            for q in range(4):
                mine = jnp.where(g == q, pb[k, :, q * ROWS : (q + 1) * ROWS], mine)
            for j in range(2):
                pair_out[j : j + 1, :] = jnp.sum(jnp.where(picked[j], mine, 0.0), axis=0, keepdims=True)
            leave(pair_out, pair_ref)

    def each(what, *orders):
        for o in orders:
            for a in range(2):
                what(a, o)

    def partials(a, o1):
        def one(k, carry):
            partial(a, o1, lax.rem(k + 2, 4))
            return carry

        lax.fori_loop(0, 4, one, 0)

    def turned(t):
        for u in range(6):
            am[t * 256 : (t + 1) * 256, u * 128 : (u + 1) * 128] = dct[t, u * 128 : (u + 1) * 128, :].T

    first(0)
    first(1)
    weights(0, 1)
    each(second, 0)
    got(("wt", 0), wbr.at[0])
    wb[1] = wb[0] + wbr[0]
    put(("wt", 1), wb.at[1], wbr.at[1], near_x)
    weights(1, 1)
    opposite(0)
    opposite(1)
    weights(0, 2)
    each(second, -1)
    weights(1, 2)
    each(second, 1)
    weights(0, 3)
    each(across, 0)
    weights(1, 3)
    each(second, 2)
    each(across, -1)
    weights(0, 4)
    each(across, 1)
    weights(1, 4)
    each(across, 2)
    weights(0, 5)
    got(("wt", 1), wbr.at[1])
    wb[2] = wb[1] + wbr[1]
    from_sibling(0)
    from_sibling(1)
    weights(1, 5)
    project(0, (1, 2, 3), True)
    weights(0, 6)
    project(1, (1, 2, 3), True)
    weights(1, 6)
    project(0, (4, 5, 6))
    weights(0, 7)
    project(1, (4, 5, 6))
    weights(1, 7)
    project(0, (7,))
    weights(0, 8)
    project(0, (8,))
    middle(0)
    begin(0, 1)
    begin(0, 2)
    weights(1, 8)
    project(1, (7, 8))
    middle(1)
    begin(1, 1)
    begin(1, 2)
    share(0)
    turned(0)
    turned(1)
    turned(2)
    partials(0, 2)
    pass_on(0, 2)
    partials(1, 2)
    each(far, 2)
    pass_on(1, 2)
    each(far, 1, 3)
    partials(0, 1)
    pass_on(0, 3)
    each(far, 0)
    partials(1, 1)
    share(1)
    pass_on(1, 3)
    partials(0, -1)
    pass_on(0, 4)
    partials(1, -1)
    each(next_to, 2)
    pass_on(1, 4)
    each(next_to, 1, 3)
    share(2)
    pass_on(0, 5)
    each(next_to, 0)
    partials(0, 0)
    pass_on(1, 5)
    partials(1, 0)
    each(here, 2)
    pass_on(0, 6)
    each(here, 1, 3)
    share(3)
    pass_on(1, 6)
    each(here, 0)
    pass_on(0, 7)
    turn(0)
    turn(1)
    share(4)
    pass_on(1, 7)
    share(5)
    pass_on(0, 8)
    finish(0, moe_ref)
    finish(1, gtok_ref)
    pass_on(1, 8)
    for e in range(2):
        for ch in range(2):
            for d in (1, -1):
                got(("r", e, 8, d, ch), zr.at[side(d), 7, pl.ds(e * EXP + ch * CHUNK, CHUNK), :])
        for base, ref in ((0, gg_ref), (128, gu_ref), (256, gd_ref)):
            rows = slice(e * EXP + base, e * EXP + base + 128)
            value = own[rows, :] + zr[0, 7, rows, :].astype(F32) + zr[1, 7, rows, :].astype(F32)
            grads_out[base // 128, e] = value if base == 256 else value.T
            leave(grads_out.at[base // 128, e], ref.at[e])

    for made in leaving:
        made.wait()
    for made in sent:
        made.wait_send()
    for a in range(2):
        for i in range(16):
            handed(a, i).wait_send()
    assert len(numbers) <= NSEM, len(numbers)


def hand_over(*refs):
    src, dst, held, sem = refs[:6], refs[6:12], refs[12:18], refs[18]
    into = [pltpu.make_async_copy(src[i], held[i], sem.at[i]) for i in range(6)]
    out = [pltpu.make_async_copy(held[i], dst[i], sem.at[6 + i]) for i in range(6)]
    for one in into:
        one.start()
    for i in range(6):
        into[i].wait()
        out[i].start()
    for one in out:
        one.wait()


def body(tokens, d_out, ids, gates, w_gate, w_up, w_down):
    anywhere = pl.BlockSpec(memory_space=pl.ANY)
    shape = jax.ShapeDtypeStruct
    moe, gtok, gg, gu, gd, pair = pl.pallas_call(
        kernel,
        out_shape=(
            shape(tokens.shape, BF16),
            shape(tokens.shape, BF16),
            shape(w_gate.shape, F32),
            shape(w_up.shape, F32),
            shape(w_down.shape, F32),
            shape(gates.shape[::-1], F32),
        ),
        in_specs=[anywhere] * 7,
        out_specs=(anywhere,) * 6,
        scratch_shapes=[
            pltpu.VMEM((2, 16, TOK, 128), BF16),
            pltpu.VMEM((16, HID, 128), BF16),
            pltpu.VMEM((3, HID, 256), F32),
            pltpu.VMEM((3, HID, 256), BF16),
            pltpu.VMEM((TOK, HID), BF16),
            pltpu.VMEM((2, EXP, 256), F32),
            pltpu.VMEM((HID, 128), F32),
            pltpu.VMEM((2, 8, HID, 128), BF16),
            pltpu.VMEM((2, 8, HID, 128), BF16),
            pltpu.VMEM((2, 16, ROWS, COLS), BF16),
            pltpu.VMEM((2, 16, ROWS, COLS), BF16),
            pltpu.VMEM((2, 16, ROWS, COLS), F32),
            pltpu.VMEM((2, 2, 4, ROWS, HALF), BF16),
            pltpu.VMEM((2, 2, 4, ROWS, HALF), BF16),
            pltpu.VMEM((2, 2, 4, ROWS, COLS), BF16),
            pltpu.VMEM((2, 2, 4, ROWS, COLS), BF16),
            pltpu.VMEM((2, 4, ROWS, COLS), F32),
            pltpu.VMEM((2, 2, ROWS, HALF), BF16),
            pltpu.VMEM((2, 2, ROWS, HALF), BF16),
            pltpu.VMEM((2, 2, ROWS, COLS), BF16),
            pltpu.VMEM((2, 2, ROWS, COLS), BF16),
            pltpu.VMEM((3, 8, TOK), F32),
            pltpu.VMEM((2, 8, TOK), F32),
            pltpu.VMEM((6, 8, TOK), F32),
            pltpu.VMEM((5, 8, TOK), F32),
            pltpu.VMEM((2, 2, 128, 128), BF16),
            pltpu.VMEM((2, ROWS), jnp.int32),
            pltpu.VMEM((2, ROWS), F32),
            pltpu.VMEM((2, ROWS, COLS), BF16),
            pltpu.VMEM((3, 2, 128, 128), F32),
            pltpu.VMEM((2, ROWS), F32),
            pltpu.SemaphoreType.DMA((NSEM,)),
            pltpu.SemaphoreType.DMA((NSEM,)),
            pltpu.SemaphoreType.DMA((12,)),
            pltpu.SemaphoreType.DMA((9,)),
        ],
        compiler_params=pltpu.CompilerParams(
            collective_id=0, has_side_effects=True, vmem_limit_bytes=58 * 2**20
        ),
    )(tokens, d_out, w_gate, w_up, w_down, ids.T, gates.T)
    made = (moe, gtok, gg, gu, gd, pair)
    moe, gtok, gg, gu, gd, pair = pl.pallas_call(
        hand_over,
        out_shape=tuple(shape(a.shape, a.dtype) for a in made),
        in_specs=[anywhere] * 6,
        out_specs=(anywhere,) * 6,
        scratch_shapes=[pltpu.VMEM(a.shape, a.dtype) for a in made] + [pltpu.SemaphoreType.DMA((12,))],
        compiler_params=pltpu.CompilerParams(vmem_limit_bytes=58 * 2**20),
    )(*made)
    return (moe, gtok, pair.T, gg, gu, gd)


def solution(mesh):
    in_specs = (
        P(("group", "blk"), "local"),
        P(("group", "blk"), "local"),
        P(("group", "blk"), None),
        P(("group", "blk"), None),
        P("group", "blk", "local"),
        P("group", "blk", "local"),
        P("group", "local", "blk"),
    )
    out_specs = (
        P(("group", "blk"), "local"),
        P(("group", "blk"), "local"),
        P(("group", "blk"), None),
        P("group", "blk", "local"),
        P("group", "blk", "local"),
        P("group", "local", "blk"),
    )
    return jax.shard_map(body, mesh=mesh, in_specs=in_specs, out_specs=out_specs, check_vma=False)
```

```python
import jax
import jax.numpy as jnp
from jax import lax
from jax.experimental import pallas as pl
from jax.experimental.pallas import tpu as pltpu
from jax.sharding import PartitionSpec as P

F32, BF16 = jnp.float32, jnp.bfloat16
MESH = pl.DeviceIdType.MESH
RX = RY = 4
RZ = 16
ROWS, COLS, HALF = 192, 256, 128
TOK = 768
HID = 768
CHUNK = 192
EXP = 384
NSEM = 280


def nt(a, b):
    return lax.dot_general(a, b, (((1,), (1,)), ((), ())), preferred_element_type=F32)


def nn(a, b):
    return jnp.dot(a, b, preferred_element_type=F32)


def side(d):
    return 0 if d == 1 else 1


def gather_chunks(s, d):
    return (0, 1) if s < RZ // 2 else ((0,) if d == 1 else (1,))


def sum_chunks(s, d):
    return (0, 1) if s > 1 else ((0,) if d == 1 else (1,))


def kernel(
    tok_ref, dout_ref, wg_ref, wu_ref, wd_ref, ids_ref, gates_ref,
    moe_ref, gtok_ref, gg_ref, gu_ref, gd_ref, pair_ref,
    tk, wall, acc, dct, am, term, own, zs, zr, ss, sr, op, s1h, r1h, s1f, r1f, op2,
    s2h, r2h, s2f, r2f, wb, wbr, pb, pbr, wtmp, ids_in, gates_in, rows_out, grads_out, pair_out,
    ssem, rsem, isem, osem,
):
    g, z, l = lax.axis_index("group"), lax.axis_index("blk"), lax.axis_index("local")
    x = lax.div(l, 4) * 2 + lax.div(g, 2)
    y, c = lax.rem(l, 4), lax.rem(g, 2)

    def place(xx, yy, cc, zz):
        return (lax.rem(xx, 2) * 2 + cc, zz, lax.div(xx, 2) * 4 + yy)

    def dev(dx=0, dy=0, dz=0, other=False):
        return place(
            lax.rem(x + dx + RX, RX), lax.rem(y + dy + RY, RY), 1 - c if other else c, lax.rem(z + dz + RZ, RZ)
        )

    sibling = dev(other=True)
    zpos = lambda by: lax.rem(z + by + 2 * RZ, RZ)
    numbers, sent = {}, []

    def number(key):
        return numbers.setdefault(key, len(numbers))

    def put(key, src, dst, to):
        i = number(key)
        made = pltpu.make_async_remote_copy(
            src_ref=src, dst_ref=dst, send_sem=ssem.at[i], recv_sem=rsem.at[i], device_id=to, device_id_type=MESH
        )
        made.start()
        sent.append(made)

    def got(key, dst):
        i = number(key)
        pltpu.make_async_remote_copy(
            src_ref=dst, dst_ref=dst, send_sem=ssem.at[i], recv_sem=rsem.at[i], device_id=sibling, device_id_type=MESH
        ).wait_recv()

    for a in range(2):
        for i in range(16):
            number(("ss", a, i))

    barrier = pltpu.get_barrier_semaphore()
    near = [sibling, dev(dx=1), dev(dx=-1), dev(dx=2), dev(dy=1), dev(dy=-1), dev(dy=2), dev(dz=1), dev(dz=-1)]
    for to in near:
        pl.semaphore_signal(barrier, inc=1, device_id=to, device_id_type=MESH)

    def along(axis, d):
        return dev(dx=d) if axis == 0 else dev(dy=d)

    def rel(a, o1, o2):
        return (o1, o2) if a == 0 else (o2, o1)

    def spot(ox, oy, cc):
        xx, yy = lax.rem(x + ox + RX, RX), lax.rem(y + oy + RY, RY)
        return lax.div(xx, 2) * 4 + yy, pl.multiple_of((lax.rem(xx, 2) * 2 + cc) * ROWS, 64)

    def block(a, o, cc=None):
        ll, row = spot(*o, c if cc is None else cc)
        return tk.at[a, pl.ds(2 * ll, 2), pl.ds(row, ROWS), :]

    def half(a, o, h):
        ll, row = spot(*o, c)
        return tk.at[a, 2 * ll + h, pl.ds(row, ROWS), :]

    row = pl.multiple_of(g * ROWS, 64)
    fetched, leaving = [], []

    def leave(src, dst):
        made = pltpu.make_async_copy(src, dst, osem.at[len(leaving)])
        made.start()
        leaving.append(made)

    def fetch(src, dst):
        made = pltpu.make_async_copy(src, dst, isem.at[len(fetched)])
        made.start()
        fetched.append(made)

    fetch(wg_ref, wtmp.at[0])
    fetch(wu_ref, wtmp.at[1])
    for e in range(2):
        fetch(wd_ref.at[e], wall.at[z, pl.ds(e * EXP + 256, 128), :])
    fetch(ids_ref, ids_in)
    fetch(gates_ref, gates_in)
    for a, ref in enumerate((tok_ref, dout_ref)):
        for h in range(2):
            fetch(ref.at[:, pl.ds(h * HALF, HALF)], tk.at[a, 2 * l + h, pl.ds(row, ROWS), :])
    for made in fetched:
        made.wait()
    for e in range(2):
        wall[z, e * EXP : e * EXP + 128, :] = wtmp[0, e].T
        wall[z, e * EXP + 128 : e * EXP + 256, :] = wtmp[1, e].T
    number_of = lax.broadcasted_iota(jnp.int32, (8, ROWS), 0)
    picked = [ids_in[k : k + 1, :] == number_of for k in range(2)]
    weights_of = jnp.where(picked[0], gates_in[0:1, :], 0.0) + jnp.where(picked[1], gates_in[1:2, :], 0.0)
    for q in range(4):
        wb[0, :, q * ROWS : (q + 1) * ROWS] = jnp.where(g == q, weights_of, 0.0)
    pb[0] = jnp.zeros((8, TOK), F32)
    pl.semaphore_wait(barrier, len(near))

    def wblock(b, e, ch):
        return wall.at[b, pl.ds(e * EXP + ch * CHUNK, CHUNK), :]

    def start_weights(e):
        for ch in range(2):
            for d in (1, -1):
                put(("w", e, 1, d, ch), wblock(z, e, ch), wblock(z, e, ch), dev(dz=d))

    start_weights(0)
    start_weights(1)
    for a in range(2):
        for d in (1, -1):
            put(("g1", a, d), block(a, (0, 0)), block(a, (0, 0)), along(a, d))
    for a in range(2):
        for d in (1, -1):
            put(("g2", a, 0, d), block(a, (0, 0)), block(a, (0, 0)), along(1 - a, d))
    put(("wt", 0), wb.at[0], wbr.at[0], sibling)
    for a in range(2):
        put(("gs", a, 0, 0), block(a, (0, 0)), block(a, (0, 0)), sibling)

    def column(a, o1):
        o = rel(a, o1, 0)
        for d in (1, -1):
            put(("g2", a, o1, d), block(a, o), block(a, o), along(1 - a, d))
        put(("gs", a, o1, 0), block(a, o), block(a, o), sibling)

    def first(a):
        for d in (1, -1):
            o, h = rel(a, -d, 0), side(d)
            got(("g1", a, d), block(a, o))
            put(("g1h", a, d), half(a, o, h), half(a, o, h), along(a, d))
        for d in (1, -1):
            column(a, -d)

    def opposite(a):
        for d in (1, -1):
            got(("g1h", a, d), half(a, rel(a, 2, 0), side(d)))
        column(a, 2)

    def second(a, o1):
        for d in (1, -1):
            o, h = rel(a, o1, -d), side(d)
            got(("g2", a, o1, d), block(a, o))
            put(("g2h", a, o1, d), half(a, o, h), half(a, o, h), along(1 - a, d))
            put(("gs", a, o1, -d), block(a, o), block(a, o), sibling)

    def across(a, o1):
        o = rel(a, o1, 2)
        for d in (1, -1):
            got(("g2h", a, o1, d), half(a, o, side(d)))
        put(("gs", a, o1, 2), block(a, o), block(a, o), sibling)

    def from_sibling(a):
        for o1 in (0, 1, -1, 2):
            for o2 in (0, 1, -1, 2):
                got(("gs", a, o1, o2), block(a, rel(a, o1, o2), 1 - c))

    def weights(e, s):
        for ch in range(2):
            for d in (1, -1):
                if ch not in gather_chunks(s, d):
                    continue
                where = wblock(zpos(-d * s), e, ch)
                got(("w", e, s, d, ch), where)
                if s < RZ // 2 and ch in gather_chunks(s + 1, d):
                    put(("w", e, s + 1, d, ch), where, where, dev(dz=d))

    def project(e, steps, fresh=False):
        pairs = [(z, zpos(8)) if s == 8 else (zpos(s), zpos(-s)) for s in steps]

        def tile(t, carry):
            rows = pl.ds(pl.multiple_of(t * 256, 256), 256)
            for a, lo, hi in ((0, e * EXP, e * EXP + 256), (1, e * EXP + 256, (e + 1) * EXP)):
                total = None if fresh else acc[t, lo:hi, :]
                for b1, b2 in pairs:
                    lhs = jnp.concatenate([wall[b1, lo:hi, :], wall[b2, lo:hi, :]], axis=1)
                    rhs = jnp.concatenate([tk[a, b1, rows, :], tk[a, b2, rows, :]], axis=1)
                    value = nt(lhs, rhs)
                    total = value if total is None else total + value
                acc[t, lo:hi, :] = total
            return carry

        lax.fori_loop(0, 3, tile, 0)

    def middle(e):
        f = [slice(e * EXP + i * 128, e * EXP + (i + 1) * 128) for i in range(3)]
        for t in range(3):
            gate, up, back = (acc[t, i, :] for i in f)
            weight = wb[2, pl.ds(2 * g + e, 1), t * 256 : (t + 1) * 256]
            s = jax.nn.sigmoid(gate)
            hidden = gate * s * up
            d_hidden = weight * back
            dct[t, f[0], :] = (d_hidden * up * s * (1.0 + gate * (1.0 - s))).astype(BF16)
            dct[t, f[1], :] = (d_hidden * gate * s).astype(BF16)
            dct[t, f[2], :] = (weight * hidden).astype(BF16)
            pair = jnp.sum(hidden * back, axis=0, keepdims=True)
            pb[0, pl.ds(2 * g + e, 1), t * 256 : (t + 1) * 256] = jnp.where(weight > 0, pair, 0.0)

    def products(e, b1, b2):
        for a, lo, hi in ((0, 0, 256), (1, 256, EXP)):
            total = None
            for t in range(3):
                rhs = jnp.concatenate(
                    [tk[a, b1, t * 256 : (t + 1) * 256, :], tk[a, b2, t * 256 : (t + 1) * 256, :]], axis=1
                )
                value = nn(dct[t, e * EXP + lo : e * EXP + hi, :], rhs)
                total = value if total is None else total + value
            term[e, lo:hi, :] = total

    def begin(e, s):
        products(e, zpos(9 - s), z if s == 1 else zpos(s - 9))
        if s == 1:
            own[e * EXP : (e + 1) * EXP, :] = term[e, :, 128:]
        for d in (1, -1):
            for ch in sum_chunks(s, d):
                if s == 1 or ch not in sum_chunks(s - 1, d):
                    step(e, s, d, ch, False)

    def step(e, s, d, ch, more):
        k = side(d)
        rows = slice(e * EXP + ch * CHUNK, e * EXP + (ch + 1) * CHUNK)
        lanes = slice(0, 128) if s == 1 else slice(k * 128, (k + 1) * 128)
        value = term[e, ch * CHUNK : (ch + 1) * CHUNK, lanes]
        if more:
            got(("r", e, s - 1, d, ch), zr.at[k, s - 2, rows, :])
            value = value + zr[k, s - 2, rows, :].astype(F32)
        zs[k, s - 1, rows, :] = value.astype(BF16)
        put(("r", e, s, d, ch), zs.at[k, s - 1, rows, :], zr.at[k, s - 1, rows, :], dev(dz=d))

    def pass_on(e, s):
        for ch in range(2):
            for d in (1, -1):
                if ch in sum_chunks(s - 1, d):
                    step(e, s, d, ch, True)
        if s < RZ // 2:
            products(e, zpos(8 - s), zpos(s - 8))

    def handed(a, i):
        k = a * 16 + i
        return pltpu.make_async_remote_copy(
            src_ref=ss.at[a, i], dst_ref=sr.at[a, i], send_sem=ssem.at[k], recv_sem=rsem.at[k],
            device_id=sibling, device_id_type=MESH,
        )

    def partial(a, o1, o2):
        i = (o1 % 4) * 4 + o2 if a == 0 else o2 * 4 + o1 % 4
        dx, dy = (o1, o2) if a == 0 else (o2, o1)
        xx, yy = lax.rem(x + dx + RX, RX), lax.rem(y + dy + RY, RY)
        ll = lax.div(xx, 2) * 4 + yy
        base = lax.rem(xx, 2) * 2
        mine = pl.ds(pl.multiple_of((base + c) * ROWS, 64), ROWS)
        theirs = pl.ds(pl.multiple_of((base + 1 - c) * ROWS, 64), ROWS)
        lo, hi = (256, EXP) if a == 0 else (0, 256)
        cols = [slice(e * EXP + lo, e * EXP + hi) for e in range(2)]
        lhs = jnp.concatenate([jnp.concatenate([am[r, k] for k in cols], axis=1) for r in (mine, theirs)], axis=0)
        rhs = jnp.concatenate(
            [jnp.concatenate([wall[2 * ll + h, k, :] for k in cols], axis=0) for h in range(2)], axis=1
        )
        value = nn(lhs, rhs)
        op[a, i] = value[:ROWS]
        ss[a, i] = value[ROWS:].astype(BF16)
        handed(a, i).start()

    def whole(a, o1, o2):
        ox, oy = rel(a, o1, o2)
        i = (ox % 4) * 4 + oy % 4
        got(("ss", a, i), sr.at[a, i])
        return op[a, i] + sr[a, i].astype(F32)

    def far(a, o2):
        value = whole(a, 2, o2).astype(BF16)
        for d in (1, -1):
            k = side(d)
            s1h[a, k, o2] = value[:, k * HALF : (k + 1) * HALF]
            put(("p1h", a, o2, d), s1h.at[a, k, o2], r1h.at[a, k, o2], along(a, d))

    def next_to(a, o2):
        for d in (1, -1):
            k = side(d)
            value = whole(a, d, o2)
            got(("p1h", a, o2, d), r1h.at[a, k, o2])
            more = r1h[a, k, o2].astype(F32)
            for h in range(2):
                part = value[:, h * HALF : (h + 1) * HALF]
                s1f[a, k, o2, :, h * HALF : (h + 1) * HALF] = (part + more if h == k else part).astype(BF16)
            put(("p1f", a, o2, d), s1f.at[a, k, o2], r1f.at[a, k, o2], along(a, d))

    def here(a, o2):
        value = whole(a, 0, o2)
        for d in (1, -1):
            got(("p1f", a, o2, d), r1f.at[a, side(d), o2])
            value = value + r1f[a, side(d), o2].astype(F32)
        op2[a, o2] = value
        if o2 == 2:
            low = value.astype(BF16)
            for d in (1, -1):
                k = side(d)
                s2h[a, k] = low[:, k * HALF : (k + 1) * HALF]
                put(("p2h", a, d), s2h.at[a, k], r2h.at[a, k], along(1 - a, d))

    def turn(a):
        for d in (1, -1):
            k = side(d)
            got(("p2h", a, d), r2h.at[a, k])
            more = r2h[a, k].astype(F32)
            for h in range(2):
                part = op2[a, d % 4, :, h * HALF : (h + 1) * HALF]
                s2f[a, k, :, h * HALF : (h + 1) * HALF] = (part + more if h == k else part).astype(BF16)
            put(("p2f", a, d), s2f.at[a, k], r2f.at[a, k], along(1 - a, d))

    def finish(a, ref):
        value = op2[a, 0]
        for d in (1, -1):
            got(("p2f", a, d), r2f.at[a, side(d)])
            value = value + r2f[a, side(d)].astype(F32)
        rows_out[a] = value.astype(BF16)
        leave(rows_out.at[a], ref)

    near_x = place(x + 1 - 2 * lax.rem(x, 2), y, c, z)
    partner = [
        sibling, near_x, dev(dx=2), place(x, y + 1 - 2 * lax.rem(y, 2), c, z), dev(dy=2),
    ]

    def share(k):
        if k:
            got(("p", k - 1), pbr.at[k - 1])
            pb[k] = pb[k - 1] + pbr[k - 1]
        if k < len(partner):
            put(("p", k), pb.at[k], pbr.at[k], partner[k])
        else:
            mine = jnp.zeros((8, ROWS), F32)
            for q in range(4):
                mine = jnp.where(g == q, pb[k, :, q * ROWS : (q + 1) * ROWS], mine)
            for j in range(2):
                pair_out[j : j + 1, :] = jnp.sum(jnp.where(picked[j], mine, 0.0), axis=0, keepdims=True)
            leave(pair_out, pair_ref)

    def each(what, *orders):
        for o in orders:
            for a in range(2):
                what(a, o)

    def partials(a, o1):
        def one(k, carry):
            partial(a, o1, lax.rem(k + 2, 4))
            return carry

        lax.fori_loop(0, 4, one, 0)

    def turned(t):
        for u in range(6):
            am[t * 256 : (t + 1) * 256, u * 128 : (u + 1) * 128] = dct[t, u * 128 : (u + 1) * 128, :].T

    first(0)
    first(1)
    weights(0, 1)
    each(second, 0)
    got(("wt", 0), wbr.at[0])
    wb[1] = wb[0] + wbr[0]
    put(("wt", 1), wb.at[1], wbr.at[1], near_x)
    weights(1, 1)
    opposite(0)
    opposite(1)
    weights(0, 2)
    each(second, -1)
    weights(1, 2)
    each(second, 1)
    weights(0, 3)
    each(across, 0)
    weights(1, 3)
    each(second, 2)
    each(across, -1)
    weights(0, 4)
    each(across, 1)
    weights(1, 4)
    each(across, 2)
    weights(0, 5)
    got(("wt", 1), wbr.at[1])
    wb[2] = wb[1] + wbr[1]
    from_sibling(0)
    from_sibling(1)
    weights(1, 5)
    project(0, (1, 2, 3), True)
    weights(0, 6)
    project(1, (1, 2, 3), True)
    weights(1, 6)
    project(0, (4, 5, 6))
    weights(0, 7)
    project(1, (4, 5, 6))
    weights(1, 7)
    project(0, (7,))
    weights(0, 8)
    project(0, (8,))
    middle(0)
    begin(0, 1)
    begin(0, 2)
    weights(1, 8)
    project(1, (7, 8))
    middle(1)
    begin(1, 1)
    begin(1, 2)
    share(0)
    turned(0)
    turned(1)
    turned(2)
    partials(0, 2)
    pass_on(0, 2)
    partials(1, 2)
    each(far, 2)
    pass_on(1, 2)
    each(far, 1, 3)
    partials(0, 1)
    pass_on(0, 3)
    each(far, 0)
    partials(1, 1)
    share(1)
    pass_on(1, 3)
    partials(0, -1)
    pass_on(0, 4)
    partials(1, -1)
    each(next_to, 2)
    pass_on(1, 4)
    each(next_to, 1, 3)
    share(2)
    pass_on(0, 5)
    each(next_to, 0)
    partials(0, 0)
    pass_on(1, 5)
    partials(1, 0)
    each(here, 2)
    pass_on(0, 6)
    each(here, 1, 3)
    share(3)
    pass_on(1, 6)
    each(here, 0)
    pass_on(0, 7)
    turn(0)
    turn(1)
    share(4)
    pass_on(1, 7)
    share(5)
    pass_on(0, 8)
    finish(0, moe_ref)
    finish(1, gtok_ref)
    pass_on(1, 8)
    for e in range(2):
        for ch in range(2):
            for d in (1, -1):
                got(("r", e, 8, d, ch), zr.at[side(d), 7, pl.ds(e * EXP + ch * CHUNK, CHUNK), :])
        for base, ref in ((0, gg_ref), (128, gu_ref), (256, gd_ref)):
            rows = slice(e * EXP + base, e * EXP + base + 128)
            value = own[rows, :] + zr[0, 7, rows, :].astype(F32) + zr[1, 7, rows, :].astype(F32)
            grads_out[base // 128, e] = value if base == 256 else value.T
            leave(grads_out.at[base // 128, e], ref.at[e])

    for made in leaving:
        made.wait()
    for made in sent:
        made.wait_send()
    for a in range(2):
        for i in range(16):
            handed(a, i).wait_send()
    assert len(numbers) <= NSEM, len(numbers)


def hand_over(*refs):
    src, dst, held, sem = refs[:6], refs[6:12], refs[12:18], refs[18]
    into = [pltpu.make_async_copy(src[i], held[i], sem.at[i]) for i in range(6)]
    out = [pltpu.make_async_copy(held[i], dst[i], sem.at[6 + i]) for i in range(6)]
    for one in into:
        one.start()
    for i in range(6):
        into[i].wait()
        out[i].start()
    for one in out:
        one.wait()


def body(tokens, d_out, ids, gates, w_gate, w_up, w_down):
    anywhere = pl.BlockSpec(memory_space=pl.ANY)
    shape = jax.ShapeDtypeStruct
    moe, gtok, gg, gu, gd, pair = pl.pallas_call(
        kernel,
        out_shape=(
            shape(tokens.shape, BF16),
            shape(tokens.shape, BF16),
            shape(w_gate.shape, F32),
            shape(w_up.shape, F32),
            shape(w_down.shape, F32),
            shape(gates.shape[::-1], F32),
        ),
        in_specs=[anywhere] * 7,
        out_specs=(anywhere,) * 6,
        scratch_shapes=[
            pltpu.VMEM((2, 16, TOK, 128), BF16),
            pltpu.VMEM((16, HID, 128), BF16),
            pltpu.VMEM((3, HID, 256), F32),
            pltpu.VMEM((3, HID, 256), BF16),
            pltpu.VMEM((TOK, HID), BF16),
            pltpu.VMEM((2, EXP, 256), F32),
            pltpu.VMEM((HID, 128), F32),
            pltpu.VMEM((2, 8, HID, 128), BF16),
            pltpu.VMEM((2, 8, HID, 128), BF16),
            pltpu.VMEM((2, 16, ROWS, COLS), BF16),
            pltpu.VMEM((2, 16, ROWS, COLS), BF16),
            pltpu.VMEM((2, 16, ROWS, COLS), F32),
            pltpu.VMEM((2, 2, 4, ROWS, HALF), BF16),
            pltpu.VMEM((2, 2, 4, ROWS, HALF), BF16),
            pltpu.VMEM((2, 2, 4, ROWS, COLS), BF16),
            pltpu.VMEM((2, 2, 4, ROWS, COLS), BF16),
            pltpu.VMEM((2, 4, ROWS, COLS), F32),
            pltpu.VMEM((2, 2, ROWS, HALF), BF16),
            pltpu.VMEM((2, 2, ROWS, HALF), BF16),
            pltpu.VMEM((2, 2, ROWS, COLS), BF16),
            pltpu.VMEM((2, 2, ROWS, COLS), BF16),
            pltpu.VMEM((3, 8, TOK), F32),
            pltpu.VMEM((2, 8, TOK), F32),
            pltpu.VMEM((6, 8, TOK), F32),
            pltpu.VMEM((5, 8, TOK), F32),
            pltpu.VMEM((2, 2, 128, 128), BF16),
            pltpu.VMEM((2, ROWS), jnp.int32),
            pltpu.VMEM((2, ROWS), F32),
            pltpu.VMEM((2, ROWS, COLS), BF16),
            pltpu.VMEM((3, 2, 128, 128), F32),
            pltpu.VMEM((2, ROWS), F32),
            pltpu.SemaphoreType.DMA((NSEM,)),
            pltpu.SemaphoreType.DMA((NSEM,)),
            pltpu.SemaphoreType.DMA((12,)),
            pltpu.SemaphoreType.DMA((9,)),
        ],
        compiler_params=pltpu.CompilerParams(
            collective_id=0, has_side_effects=True, vmem_limit_bytes=58 * 2**20
        ),
    )(tokens, d_out, w_gate, w_up, w_down, ids.T, gates.T)
    made = (moe, gtok, gg, gu, gd, pair)
    moe, gtok, gg, gu, gd, pair = pl.pallas_call(
        hand_over,
        out_shape=tuple(shape(a.shape, a.dtype) for a in made),
        in_specs=[anywhere] * 6,
        out_specs=(anywhere,) * 6,
        scratch_shapes=[pltpu.VMEM(a.shape, a.dtype) for a in made] + [pltpu.SemaphoreType.DMA((12,))],
        compiler_params=pltpu.CompilerParams(vmem_limit_bytes=58 * 2**20),
    )(*made)
    return (moe, gtok, pair.T, gg, gu, gd)


def solution(mesh):
    in_specs = (
        P(("group", "blk"), "local"),
        P(("group", "blk"), "local"),
        P(("group", "blk"), None),
        P(("group", "blk"), None),
        P("group", "blk", "local"),
        P("group", "blk", "local"),
        P("group", "local", "blk"),
    )
    out_specs = (
        P(("group", "blk"), "local"),
        P(("group", "blk"), "local"),
        P(("group", "blk"), None),
        P("group", "blk", "local"),
        P("group", "blk", "local"),
        P("group", "local", "blk"),
    )
    return jax.shard_map(body, mesh=mesh, in_specs=in_specs, out_specs=out_specs, check_vma=False)
```
